512 devices in a mesh: grp: 16 (over z), ctx: 32 (over x, y, core).
Axes of the slice: x: 4, y: 4, z: 16, core: 2. Of those that a mesh axis runs over, the one named last changes fastest.
Arguments:
- query: bfloat16 [2048, 128, 192], P('grp', 'ctx'), may hold values from -44 to 44
- absorb_k: bfloat16 [128, 128, 512], P('ctx'), may hold values from -0.5 to 0.5
- absorb_v: bfloat16 [128, 512, 128], P('ctx'), may hold values from -0.25 to 0.25
- latent_cache: bfloat16 [32768, 576], P('ctx'), may hold values from -6 to 6
- cold_blocks: int32 [2048, 30], P(('grp', 'ctx')), may hold values from 0 to 509, as said below
Outputs:
- attended: bfloat16 [2048, 128, 128], P('grp', 'ctx')
The draws below stay inside these ranges and needn't reach their ends.
Inputs may be any that keep to these rules, and one draw needn't show every extreme that they name: `cold_blocks`: each row names 30 distinct blocks, none of the newest 2. Over the 4 rows of one device (aligned groups of rows in order), at most 2 distinct named blocks lie in the 16 blocks of any one ctx index; the share of the last ctx index reaches 2 in every such group.
All inputs are finite; a program needn't handle non-finite values.
Results may differ from the reference program's by a relative error of at most 0.0067.
Values may be sent and summed in bfloat16 or wider, within the bound.
A program may use at most 64 MiB of HBM per device.

```python
import math
import jax
import jax.numpy as jnp
from jax import lax

H = 128
DL = 512
DR = 64
DN = 128
DV = 128
BLK = 64
TOPB = 32
HOT = 2
Q_DEV = 4
QROWS = 2048
CONTEXT = 32768
BPD = 16
NBLK = 512
COLD = 2
N_CTX = 32


def draw_query(key, part):
    key = jax.random.fold_in(key, 1)
    base = jnp.clip(jax.random.normal(key, (QROWS, H, DN + DR), jnp.float32), -6.0, 6.0)
    return base.astype(jnp.bfloat16)


def draw_latent_cache(key, part):
    key = jax.random.fold_in(key, 2)
    base = jnp.clip(jax.random.normal(key, (CONTEXT, DL + DR), jnp.float32), -6.0, 6.0)
    return base.astype(jnp.bfloat16)


def draw_cold_blocks(key, part):
    key = jax.random.fold_in(key, 3)
    ndev = QROWS // Q_DEV
    ncand = N_CTX * COLD
    keep = TOPB - HOT
    key_a, key_b, key_c, key_d, key_e = jax.random.split(key, 5)
    owner_keys = jax.random.split(key_a, ndev * N_CTX)
    perms = jax.vmap(lambda k: jax.random.permutation(k, BPD))(owner_keys)
    cands = perms[:, :COLD].reshape(ndev, N_CTX, COLD)
    newest_keys = jax.random.split(key_b, ndev)
    newest = jax.vmap(lambda k: jax.random.permutation(k, BPD - HOT))(newest_keys)[:, :COLD]
    cands = cands.at[:, N_CTX - 1, :].set(newest)
    owners = jnp.arange(N_CTX, dtype=jnp.int32)[None, :, None] * BPD
    gids = (owners + cands).reshape(ndev, ncand).astype(jnp.int32)
    row_keys = jax.random.split(key_c, ndev * Q_DEV)
    idx = jax.vmap(lambda k: jax.random.permutation(k, ncand))(row_keys)[:, :keep].reshape(ndev, Q_DEV, keep)
    first_keys = jax.random.split(key_d, ndev)
    others = jax.vmap(lambda k: jax.random.permutation(k, ncand - COLD))(first_keys)[:, :keep - COLD]
    tail = jnp.broadcast_to(jnp.arange(ncand - COLD, ncand, dtype=jnp.int32)[None, :], (ndev, COLD))
    first = jnp.concatenate([tail, others.astype(jnp.int32)], axis=1)
    order_keys = jax.random.split(key_e, ndev)
    order = jax.vmap(lambda k: jax.random.permutation(k, keep))(order_keys)
    first = jnp.take_along_axis(first, order, axis=1)
    idx = idx.astype(jnp.int32).at[:, 0, :].set(first)
    picked = jnp.take_along_axis(jnp.broadcast_to(gids[:, None, :], (ndev, Q_DEV, ncand)), idx, axis=2)
    return picked.reshape(QROWS, keep).astype(jnp.int32)


def block_levels(stream_key, extent, shards, least, top_value):
    gain = 1.0
    for axis_at, shards_of in shards:
        steps = jax.random.uniform(jax.random.fold_in(jax.random.fold_in(stream_key, 6), axis_at), (shards_of,), jnp.float32, least / len(shards), top_value / len(shards))
        gain = gain * jnp.repeat(jnp.exp(steps), extent[axis_at] // shards_of).reshape((-1,) + (1,) * (len(extent) - 1 - axis_at))
    return gain


def gaussian(rng, shape, scale, reach, cuts=(), kind=jnp.bfloat16):
    gain = block_levels(rng, shape, cuts, -0.22, 0.18) if cuts else 1.0
    result = jax.random.normal(rng, shape, jnp.float32) * scale * gain
    return jnp.minimum(jnp.maximum(result, -reach), reach).astype(kind)


def setup_inputs(seed: int = 0) -> dict:
    splits = jax.random.split(jax.random.key(seed), 6)
    return {
        "query": draw_query(jax.random.fold_in(splits[5], 71), 0),
        "absorb_k": gaussian(splits[1], (H, DN, DL), DN ** -0.5, 0.5, ((0, 32),)),
        "absorb_v": gaussian(splits[2], (H, DL, DV), DL ** -0.5, 0.25, ((0, 32),)),
        "latent_cache": draw_latent_cache(jax.random.fold_in(splits[5], 71), 0),
        "cold_blocks": draw_cold_blocks(jax.random.fold_in(splits[5], 71), 0),
    }


def reference(query, absorb_k, absorb_v, latent_cache, cold_blocks):
    q_lat = jnp.einsum('rhn,hnl->rhl', query[:, :, :DN].astype(jnp.float32), absorb_k.astype(jnp.float32))
    q_full = jnp.concatenate([q_lat, query[:, :, DN:].astype(jnp.float32)], axis=-1).astype(jnp.bfloat16)
    newest = NBLK - HOT + jnp.arange(HOT, dtype=jnp.int32)
    picks = jnp.concatenate([jnp.broadcast_to(newest[None, :], (cold_blocks.shape[0], HOT)), cold_blocks.astype(jnp.int32)], axis=1)
    scale = 1.0 / math.sqrt(DN + DR)
    offsets = jnp.arange(BLK, dtype=jnp.int32)

    def one_row(items):
        q_row, pick_row = items
        tokens = (pick_row[:, None] * BLK + offsets[None, :]).reshape(-1).astype(jnp.int32)
        keys = jnp.take(latent_cache, tokens, axis=0)
        scores = jnp.dot(q_row, keys.T, preferred_element_type=jnp.float32) * scale
        highest = lax.optimization_barrier(jnp.max(scores, axis=-1, keepdims=True))
        weights = jnp.exp(scores - highest)
        probs = (weights / lax.optimization_barrier(jnp.sum(weights, axis=-1, keepdims=True))).astype(jnp.bfloat16)
        return jnp.dot(probs, keys[:, :DL], preferred_element_type=jnp.float32).astype(jnp.bfloat16)
    out_lat = lax.map(one_row, (q_full, picks))
    attended = jnp.einsum('rhl,hlv->rhv', out_lat.astype(jnp.float32), absorb_v.astype(jnp.float32))
    return attended.astype(jnp.bfloat16)
```

```python
import functools
import math

import jax
import jax.numpy as jnp
from jax import lax
from jax.experimental import pallas as pl
from jax.experimental.pallas import tpu as pltpu
from jax.sharding import PartitionSpec as P

MESH = pl.DeviceIdType.MESH
DL = 512
DN = 128
BLK = 64
ROWS = 144
N = 32
NEG = -1e30

RINGS = (
    ((2, 2),),
    ((2, 1), (2, 3), (1, 2), (3, 2)),
    ((2, 0), (0, 2)),
    ((1, 1), (3, 3), (1, 3), (3, 1)),
    ((1, 0), (3, 0), (0, 1), (0, 3)),
)
OFFSETS = [(0, 0, 0)]
for ring in RINGS:
    for core in (0, 1):
        OFFSETS += [(dx, dy, core) for dx, dy in ring]
OFFSETS.append((0, 0, 1))


def ahead(me, offset):
    dx, dy, dc = offset
    x, y, c = me // 8, (me // 2) % 4, me % 2
    return (((x + dx) % 4) * 4 + (y + dy) % 4) * 2 + (c + dc) % 2


def behind(me, offset):
    dx, dy, dc = offset
    return ahead(me, ((4 - dx) % 4, (4 - dy) % 4, dc))


def to(device):
    return dict(device_id={"ctx": device}, device_id_type=MESH)


def pack(cache, rope, id0, id1, put):
    put(pl.ds(0, BLK), pl.ds(0, DL), cache[id0, :, :DL])
    put(pl.ds(BLK, BLK), pl.ds(0, DL), cache[id1, :, :DL])
    lane = lax.broadcasted_iota(jnp.int32, (BLK, 128), 1)
    both = jnp.where(lane < 64, rope[id0], rope[id1])
    for k in range(4):
        put(pl.ds(2 * BLK, 16), pl.ds(128 * k, 128), both[16 * k : 16 * k + 16])


def kernel(
    query, absorb_k, absorb_v, cache, cold, out,
    rope, ids_out, ids_in, ids, bias, q_out, q_all, stage, keys, hot, extra,
    top, total, acc, lat_out, lat_in,
    ids_ss, ids_rs, q_ss, q_rs, k_ss, k_rs, o_ss, o_rs, hot_ss, hot_rs, id_sem,
):
    me = lax.axis_index("ctx")
    x, y, c = me // 8, (me // 2) % 4, me % 2
    barrier = pltpu.get_barrier_semaphore()
    for p in range(1, N):
        pl.semaphore_signal(barrier, inc=1, **to(ahead(me, OFFSETS[p])))

    base = lax.broadcasted_iota(jnp.int32, (N, 1), 0) * 16
    local = [cold[r : r + 1, :] - base for r in range(4)]
    low, high = None, None
    for r in range(4):
        inside = (local[r] >= 0) & (local[r] < 16)
        a = jnp.min(jnp.where(inside, local[r], 99), axis=1, keepdims=True)
        b = jnp.max(jnp.where(inside, local[r], -1), axis=1, keepdims=True)
        low = a if r == 0 else jnp.minimum(low, a)
        high = b if r == 0 else jnp.maximum(high, b)
    id0 = jnp.where(high < 0, 0, low)
    id1 = jnp.where(high < 0, 0, high)
    lane = lax.broadcasted_iota(jnp.int32, (N, 128), 1)
    ids_out[...] = jnp.where(lane == 0, id0, id1).reshape(N, 1, 128)
    for s, wanted in ((0, id0), (1, id1)):
        mark = jnp.zeros((N, 128), jnp.float32)
        for r in range(4):
            found = jnp.max(jnp.where(local[r] == wanted, 1, 0), axis=1, keepdims=True)
            if s == 1:
                found = jnp.where(id1 == id0, 0, found)
            mark = jnp.where((lane == r) & (found == 0), NEG, mark)
        bias[s] = mark

    pl.semaphore_wait(barrier, N - 1)
    id_copies = []
    for p in range(1, N):
        dst = ahead(me, OFFSETS[p])
        copy = pltpu.make_async_remote_copy(
            src_ref=ids_out.at[dst], dst_ref=ids_in.at[p], send_sem=ids_ss.at[p], recv_sem=ids_rs.at[p], **to(dst)
        )
        copy.start()
        id_copies.append(copy)

    doubled = jnp.concatenate([cache[:, :, DL:], cache[:, :, DL:]], axis=2)
    rope[...] = doubled

    def hot_copy(k, offset):
        return pltpu.make_async_remote_copy(
            src_ref=hot, dst_ref=hot, send_sem=hot_ss.at[k], recv_sem=hot_rs, **to(ahead(me, offset))
        )

    across = [hot_copy(d - 1, (d, 0, 0)) for d in (1, 2, 3)]
    down = [hot_copy(d + 2, (0, d, 0)) for d in (1, 2, 3)]
    over = hot_copy(6, (0, 0, 1))

    def put_hot(rows, columns, values):
        hot[rows, columns] = values

    @pl.when(me == N - 1)
    def _():
        pack(cache, rope, 14, 15, put_hot)
        for copy in across + down:
            copy.start()

    head = lax.broadcasted_iota(jnp.int32, (512, DN), 0) % 4
    plain = query[:, :DN]
    zero = jnp.zeros_like(plain)
    spread = jnp.concatenate([jnp.where(head == h, plain, zero) for h in range(4)], axis=1)
    q_out[:, :DL] = jnp.dot(spread, absorb_k[...], preferred_element_type=jnp.float32).astype(jnp.bfloat16)
    turn = query[:, DN:]
    q_out[:, DL:] = jnp.concatenate([turn, turn], axis=1)
    q_copies = []
    for p in range(1, N):
        dst = ahead(me, OFFSETS[p])
        copy = pltpu.make_async_remote_copy(
            src_ref=q_out.at[pl.ds(pl.multiple_of(dst * 16, 16), 16)],
            dst_ref=q_all.at[pl.ds(pl.multiple_of(me * 16, 16), 16), pl.ds(0, 640)],
            send_sem=q_ss.at[p], recv_sem=q_rs.at[p], **to(dst)
        )
        copy.start()
        q_copies.append(copy)

    @pl.when((y == 3) & (c == 1) & (x != 3))
    def _():
        across[0].wait_recv()
        for copy in down:
            copy.start()

    for p in range(1, N):
        id_copies[p - 1].wait_recv()
    fetch = pltpu.make_async_copy(ids_in, ids, id_sem)
    fetch.start()
    fetch.wait()
    k_copies = []
    for p in range(1, N):
        q = OFFSETS.index(((4 - OFFSETS[p][0]) % 4, (4 - OFFSETS[p][1]) % 4, OFFSETS[p][2]))
        dst = behind(me, OFFSETS[q])

        def put(rows, columns, values, p=p):
            stage[p, rows, columns] = values

        pack(cache, rope, ids[q, 0, 0], ids[q, 0, 1], put)
        copy = pltpu.make_async_remote_copy(
            src_ref=stage.at[p], dst_ref=keys.at[p], send_sem=k_ss.at[p], recv_sem=k_rs.at[p], **to(dst)
        )
        copy.start()
        k_copies.append(copy)

    @pl.when((c == 1) & (y != 3))
    def _():
        down[0].wait_recv()

    @pl.when(c == 1)
    def _():
        over.start()

    mine = pltpu.make_async_copy(ids_out.at[pl.ds(me, 1)], ids.at[pl.ds(0, 1)], id_sem)
    mine.start()
    mine.wait()

    def put_own(rows, columns, values):
        keys[0, rows, columns] = values

    pack(cache, rope, ids[0, 0, 0], ids[0, 0, 1], put_own)
    own = pl.ds(pl.multiple_of(me * 16, 16), 16)
    q_all[own, pl.ds(0, 640)] = q_out[own, :]
    marks = (lax.broadcasted_iota(jnp.int32, (512, 128), 0) // 4) % 4 == lax.broadcasted_iota(
        jnp.int32, (512, 128), 1
    )
    q_all[:, 640:] = jnp.where(marks, 1.0, 0.0).astype(jnp.bfloat16)
    for p in range(1, N):
        q_copies[p - 1].wait_recv()

    scale = math.log2(math.e) / math.sqrt(192)
    half = lax.broadcasted_iota(jnp.int32, (BLK, 128), 1) < 64
    none = jnp.zeros((BLK, 128), jnp.bfloat16)

    def unpack(tile, at, b0, b1):
        both = jnp.concatenate([tile[:, 128 * k : 128 * k + 128] for k in range(4)], axis=0)
        extra[pl.ds(at, BLK), pl.ds(0, 128)] = jnp.where(half, both, none)
        extra[pl.ds(at + BLK, BLK), pl.ds(0, 128)] = jnp.where(half, none, both)
        extra[pl.ds(at, BLK), pl.ds(128, 128)] = b0
        extra[pl.ds(at + BLK, BLK), pl.ds(128, 128)] = b1

    def scores(latent, tokens):
        dims = (((1,), (1,)), ((), ()))
        s = lax.dot_general(q_all[:, :DL], latent, dims, preferred_element_type=jnp.float32)
        s += lax.dot_general(q_all[:, DL:], extra[:tokens], dims, preferred_element_type=jnp.float32)
        return s * scale

    def add(latent, tokens):
        s = scores(latent, tokens)
        old = top[...]
        new = jnp.maximum(old, jnp.max(s, axis=1, keepdims=True))
        fade = jnp.exp2(old - new)
        w = jnp.exp2(s - new)
        total[...] = total[...] * fade + jnp.sum(w, axis=1, keepdims=True)
        top[...] = new
        acc[...] = acc[...] * fade + jnp.dot(
            w.astype(jnp.bfloat16), latent, preferred_element_type=jnp.float32
        )

    top[...] = jnp.full((512, 1), NEG, jnp.float32)
    total[...] = jnp.zeros((512, 1), jnp.float32)
    acc[...] = jnp.zeros((512, DL), jnp.float32)
    for chunk in range(8):
        for j in range(4):
            p = 4 * chunk + j
            if p:
                k_copies[p - 1].wait_recv()
            owner = behind(me, OFFSETS[p])
            b0 = jnp.broadcast_to(bias[0, pl.ds(owner, 1), :], (BLK, 128)).astype(jnp.bfloat16)
            b1 = jnp.broadcast_to(bias[1, pl.ds(owner, 1), :], (BLK, 128)).astype(jnp.bfloat16)
            unpack(keys[p, pl.ds(128, 16), :], 128 * j, b0, b1)
        add(keys[pl.ds(4 * chunk, 4), pl.ds(0, 128), :].reshape(512, DL), 512)
        if chunk == 0:
            @pl.when(c == 0)
            def _():
                over.wait_recv()

            unpack(hot[pl.ds(128, 16), :], 0, none, none)
            add(hot[pl.ds(0, 128), :], 128)

    lat_out[...] = (acc[...] / total[...]).astype(jnp.bfloat16)
    o_copies = []
    for p in range(1, N):
        dst = ahead(me, OFFSETS[p])
        copy = pltpu.make_async_remote_copy(
            src_ref=lat_out.at[pl.ds(pl.multiple_of(dst * 16, 16), 16)],
            dst_ref=lat_in.at[pl.ds(pl.multiple_of(me * 16, 16), 16)],
            send_sem=o_ss.at[p], recv_sem=o_rs.at[p], **to(dst)
        )
        copy.start()
        o_copies.append(copy)
    lat_in[own, :] = lat_out[own, :]
    for p in range(1, N):
        o_copies[p - 1].wait_recv()
    got = lat_in[...]
    result = jnp.zeros((512, 128), jnp.float32)
    for h in range(4):
        result = jnp.where(head == h, jnp.dot(got, absorb_v[h], preferred_element_type=jnp.float32), result)
    out[...] = result.astype(jnp.bfloat16)

    for copies in (id_copies, q_copies, k_copies, o_copies):
        for copy in copies:
            copy.wait_send()

    @pl.when(me == N - 1)
    def _():
        for copy in across:
            copy.wait_send()

    @pl.when((y == 3) & (c == 1))
    def _():
        for copy in down:
            copy.wait_send()

    @pl.when(c == 1)
    def _():
        over.wait_send()


def body(query, absorb_k, absorb_v, latent_cache, cold_blocks):
    vmem = pl.BlockSpec(memory_space=pltpu.VMEM)
    bf16, f32, i32 = jnp.bfloat16, jnp.float32, jnp.int32
    dma = pltpu.SemaphoreType.DMA
    out = pl.pallas_call(
        kernel,
        out_shape=jax.ShapeDtypeStruct((512, 128), bf16),
        in_specs=[vmem] * 5,
        out_specs=vmem,
        scratch_shapes=[
            pltpu.VMEM((16, BLK, 128), bf16),
            pltpu.VMEM((N, 1, 128), i32),
            pltpu.VMEM((N, 1, 128), i32),
            pltpu.SMEM((N, 1, 128), i32),
            pltpu.VMEM((2, N, 128), f32),
            pltpu.VMEM((512, 640), bf16),
            pltpu.VMEM((512, 768), bf16),
            pltpu.VMEM((N, ROWS, DL), bf16),
            pltpu.VMEM((N, ROWS, DL), bf16),
            pltpu.VMEM((ROWS, DL), bf16),
            pltpu.VMEM((512, 256), bf16),
            pltpu.VMEM((512, 1), f32),
            pltpu.VMEM((512, 1), f32),
            pltpu.VMEM((512, DL), f32),
            pltpu.VMEM((512, DL), bf16),
            pltpu.VMEM((512, DL), bf16),
        ]
        + [dma((N,))] * 8
        + [dma((7,)), dma, dma],
        compiler_params=pltpu.CompilerParams(collective_id=0, has_side_effects=True, vmem_limit_bytes=48 * 2**20),
    )(
        query.reshape(512, 192),
        absorb_k.reshape(512, DL),
        absorb_v,
        latent_cache.reshape(16, BLK, 576),
        cold_blocks,
    )
    return out.reshape(128, 4, 128)


def solution(mesh):
    placed = (
        P("grp", "ctx", None),
        P("ctx", None, None),
        P("ctx", None, None),
        P("ctx", None),
        P(("grp", "ctx"), None),
    )
    return jax.shard_map(
        body, mesh=mesh, in_specs=placed, out_specs=P("grp", "ctx", None), check_vma=False
    )
```

```python
import functools
import math

import jax
import jax.numpy as jnp
from jax import lax
from jax.experimental import pallas as pl
from jax.experimental.pallas import tpu as pltpu
from jax.sharding import PartitionSpec as P

MESH = pl.DeviceIdType.MESH
DL = 512
DN = 128
BLK = 64
QUARTER = 32
PARTS = 4
N = 32
NEG = -1e30

RINGS = (
    ((1, 1), (3, 3), (1, 3), (3, 1)),
    ((2, 1), (0, 1), (2, 3), (0, 3)),
    ((2, 2),),
    ((1, 2), (1, 0), (3, 2), (3, 0)),
    ((2, 0), (0, 2)),
)
OFFSETS = [(0, 0, 0)]
for ring in RINGS:
    for core in (0, 1):
        OFFSETS += [(dx, dy, core) for dx, dy in ring]
OFFSETS.append((0, 0, 1))


def ahead(me, offset):
    dx, dy, dc = offset
    x, y, c = me // 8, (me // 2) % 4, me % 2
    return (((x + dx) % 4) * 4 + (y + dy) % 4) * 2 + (c + dc) % 2


def behind(me, offset):
    dx, dy, dc = offset
    return ahead(me, ((4 - dx) % 4, (4 - dy) % 4, dc))


def to(device):
    return dict(device_id={"ctx": device}, device_id_type=MESH)


def pack(cache, rope, id0, id1, latents, turns):
    for k in range(PARTS):
        latents[k][...] = cache[id0 if k < 2 else id1, pl.ds(QUARTER * (k % 2), QUARTER), :]
    lane = lax.broadcasted_iota(jnp.int32, (BLK, 128), 1)
    both = jnp.where(lane < 64, rope[id0], rope[id1])
    for b in range(4):
        turns[:, pl.ds(128 * b, 128)] = both[16 * b : 16 * b + 16]


def kernel(
    query_at, absorb_k_at, absorb_v_at, stored_at, cold, out,
    query, absorb_k, absorb_v, stored,
    cache, rope, ids_out, ids_in, ids, bias, q_out, q_all, stage, stage_turn, keys, keys_turn, hot, hot_turn, extra,
    top, total, acc, lat_out, lat_in,
    ids_ss, ids_rs, q_ss, q_rs, k_ss, k_rs, t_ss, t_rs, o_ss, o_rs, hot_ss, hot_rs, id_sem, in_sem,
):
    me = lax.axis_index("ctx")
    x, y, c = me // 8, (me // 2) % 4, me % 2
    barrier = pltpu.get_barrier_semaphore()
    for p in range(1, N):
        pl.semaphore_signal(barrier, inc=1, **to(ahead(me, OFFSETS[p])))

    loads = [
        pltpu.make_async_copy(src, dst, in_sem.at[k])
        for k, (src, dst) in enumerate(
            ((stored_at, stored), (query_at, query), (absorb_k_at, absorb_k), (absorb_v_at, absorb_v))
        )
    ]
    for load in loads:
        load.start()

    base = lax.broadcasted_iota(jnp.int32, (N, 1), 0) * 16
    local = [cold[r : r + 1, :] - base for r in range(4)]
    low, high = None, None
    for r in range(4):
        inside = (local[r] >= 0) & (local[r] < 16)
        a = jnp.min(jnp.where(inside, local[r], 99), axis=1, keepdims=True)
        b = jnp.max(jnp.where(inside, local[r], -1), axis=1, keepdims=True)
        low = a if r == 0 else jnp.minimum(low, a)
        high = b if r == 0 else jnp.maximum(high, b)
    id0 = jnp.where(high < 0, 0, low)
    id1 = jnp.where(high < 0, 0, high)
    lane = lax.broadcasted_iota(jnp.int32, (N, 128), 1)
    ids_out[...] = jnp.where(lane == 0, id0, id1).reshape(N, 1, 128)
    for s, wanted in ((0, id0), (1, id1)):
        mark = jnp.zeros((N, 128), jnp.float32)
        for r in range(4):
            found = jnp.max(jnp.where(local[r] == wanted, 1, 0), axis=1, keepdims=True)
            if s == 1:
                found = jnp.where(id1 == id0, 0, found)
            mark = jnp.where((lane == r) & (found == 0), NEG, mark)
        bias[s] = mark

    pl.semaphore_wait(barrier, N - 1)
    for p in range(1, N):
        dst = ahead(me, OFFSETS[p])
        pltpu.make_async_remote_copy(
            src_ref=ids_out.at[dst], dst_ref=ids_in.at[p], send_sem=ids_ss, recv_sem=ids_rs, **to(dst)
        ).start()

    def settled(ref, sends, lands):
        return pltpu.make_async_remote_copy(src_ref=ref, dst_ref=ref, send_sem=sends, recv_sem=lands, **to(ahead(me, OFFSETS[1])))

    lanes = (((1,), (1,)), ((), ()))
    unit = jnp.where(
        lax.broadcasted_iota(jnp.int32, (256, 256), 0) == lax.broadcasted_iota(jnp.int32, (256, 256), 1), 1.0, 0.0
    ).astype(jnp.bfloat16)
    loads[0].wait()
    for k in range(4):
        part = pl.ds(256 * k, 256)
        turned = lax.dot_general(unit, stored[:DL, part], lanes, preferred_element_type=jnp.float32)
        cache[pl.ds(4 * k, 4)] = turned.astype(jnp.bfloat16).reshape(4, BLK, DL)
        tail = stored[DL:, part]
        turned = lax.dot_general(
            unit, jnp.concatenate([tail, tail], axis=0), lanes, preferred_element_type=jnp.float32
        )
        rope[pl.ds(4 * k, 4)] = turned.astype(jnp.bfloat16).reshape(4, BLK, 128)

    def hot_copies(k, offset):
        device = to(ahead(me, offset))
        return [
            pltpu.make_async_remote_copy(
                src_ref=ref, dst_ref=ref, send_sem=hot_ss.at[i, k], recv_sem=hot_rs.at[i], **device
            )
            for i, ref in enumerate((hot, hot_turn))
        ]

    across = hot_copies(0, (1, 0, 0)) + hot_copies(1, (2, 0, 0)) + hot_copies(2, (3, 0, 0))
    down = hot_copies(3, (0, 1, 0)) + hot_copies(4, (0, 2, 0)) + hot_copies(5, (0, 3, 0))
    over = hot_copies(6, (0, 0, 1))

    @pl.when(me == N - 1)
    def _():
        pack(cache, rope, 14, 15, [hot.at[k] for k in range(PARTS)], hot_turn)
        for copy in across + down:
            copy.start()

    row = lax.broadcasted_iota(jnp.int32, (512, 128), 0)
    column = lax.broadcasted_iota(jnp.int32, (512, 128), 1)
    plain, turn = [], None
    loads[1].wait()
    loads[2].wait()
    for h in range(4):
        pick = jnp.where(row == 4 * column + h, 1.0, 0.0).astype(jnp.bfloat16)
        spread = lax.dot_general(pick, query[h], lanes, preferred_element_type=jnp.float32)
        plain.append(spread[:, :DN].astype(jnp.bfloat16))
        turn = spread[:, DN:] if h == 0 else turn + spread[:, DN:]
    q_out[:, :DL] = jnp.dot(
        jnp.concatenate(plain, axis=1), absorb_k[...], preferred_element_type=jnp.float32
    ).astype(jnp.bfloat16)
    turn = turn.astype(jnp.bfloat16)
    q_out[:, DL:] = jnp.concatenate([turn, turn], axis=1)
    for p in range(1, N):
        dst = ahead(me, OFFSETS[p])
        pltpu.make_async_remote_copy(
            src_ref=q_out.at[pl.ds(pl.multiple_of(dst * 16, 16), 16)],
            dst_ref=q_all.at[pl.ds(16 * p, 16), pl.ds(0, 640)],
            send_sem=q_ss, recv_sem=q_rs, **to(dst)
        ).start()

    settled(ids_in.at[pl.ds(1, N - 1)], ids_ss, ids_rs).wait_recv()
    fetch = pltpu.make_async_copy(ids_in, ids, id_sem)
    fetch.start()
    fetch.wait()

    def send_part(k, p):
        pltpu.make_async_remote_copy(
            src_ref=stage.at[k, p], dst_ref=keys.at[k, p], send_sem=k_ss.at[k], recv_sem=k_rs.at[k, p // 16],
            **to(ahead(me, OFFSETS[p]))
        ).start()

    for p in range(1, N):
        q = OFFSETS.index(((4 - OFFSETS[p][0]) % 4, (4 - OFFSETS[p][1]) % 4, OFFSETS[p][2]))
        pack(
            cache, rope, ids[q, 0, 0], ids[q, 0, 1], [stage.at[k, p] for k in range(PARTS)], stage_turn.at[p]
        )
        pltpu.make_async_remote_copy(
            src_ref=stage_turn.at[p], dst_ref=keys_turn.at[p], send_sem=t_ss, recv_sem=t_rs,
            **to(ahead(me, OFFSETS[p]))
        ).start()
        send_part(0, p)

    @pl.when((y == 3) & (c == 1) & (x != 3))
    def _():
        for copy in across[:2]:
            copy.wait_recv()
        for copy in down:
            copy.start()

    for p in range(1, N):
        send_part(1, p)

    @pl.when((c == 1) & (y != 3))
    def _():
        for copy in down[:2]:
            copy.wait_recv()

    @pl.when(c == 1)
    def _():
        for copy in over:
            copy.start()

    for k in (2, 3):
        for p in range(1, N):
            send_part(k, p)

    mine = pltpu.make_async_copy(ids_out.at[pl.ds(me, 1)], ids.at[pl.ds(0, 1)], id_sem)
    mine.start()
    mine.wait()

    pack(cache, rope, ids[0, 0, 0], ids[0, 0, 1], [keys.at[k, 0] for k in range(PARTS)], keys_turn.at[0])
    own = pl.ds(pl.multiple_of(me * 16, 16), 16)
    q_all[pl.ds(0, 16), pl.ds(0, 640)] = q_out[own, :]
    marks = (lax.broadcasted_iota(jnp.int32, (512, 128), 0) // 4) % 4 == lax.broadcasted_iota(
        jnp.int32, (512, 128), 1
    )
    q_all[:, 640:] = jnp.where(marks, 1.0, 0.0).astype(jnp.bfloat16)
    for p in range(N):
        owner = behind(me, OFFSETS[p])
        for s in range(2):
            wide = jnp.broadcast_to(bias[s, pl.ds(owner, 1), :], (QUARTER, 128)).astype(jnp.bfloat16)
            for k in (2 * s, 2 * s + 1):
                extra[k, p, :, pl.ds(128, 128)] = wide
    settled(q_all.at[pl.ds(16, 496), pl.ds(0, 640)], q_ss, q_rs).wait_recv()

    scale = math.log2(math.e) / math.sqrt(192)
    first = lax.broadcasted_iota(jnp.int32, (QUARTER, 128), 1) < 64
    none = jnp.zeros((QUARTER, 128), jnp.bfloat16)

    def unpack(turns, put):
        for b in range(2):
            both = jnp.concatenate([turns[:, 256 * b + 128 * i : 256 * b + 128 * i + 128] for i in range(2)], axis=0)
            put(b, jnp.where(first, both, none))
            put(2 + b, jnp.where(first, none, both))

    def scores(latent, more):
        s = lax.dot_general(q_all[:, :DL], latent, lanes, preferred_element_type=jnp.float32)
        s += lax.dot_general(q_all[:, DL:], more, lanes, preferred_element_type=jnp.float32)
        return s * scale

    def add(latent, more):
        s = scores(latent, more)
        old = top[...]
        new = jnp.maximum(old, jnp.max(s, axis=1, keepdims=True))
        fade = jnp.exp2(old - new)
        w = jnp.exp2(s - new)
        total[...] = total[...] * fade + jnp.sum(w, axis=1, keepdims=True)
        top[...] = new
        acc[...] = acc[...] * fade + jnp.dot(
            w.astype(jnp.bfloat16), latent, preferred_element_type=jnp.float32
        )

    top[...] = jnp.full((512, 1), NEG, jnp.float32)
    total[...] = jnp.zeros((512, 1), jnp.float32)
    acc[...] = jnp.zeros((512, DL), jnp.float32)

    @pl.when(c == 0)
    def _():
        for copy in over:
            copy.wait_recv()

    hot_more = []
    unpack(hot_turn[...], lambda k, values: hot_more.append((k, values)))
    hot_more = jnp.concatenate([values for _, values in sorted(hot_more, key=lambda item: item[0])], axis=0)
    add(hot[...].reshape(128, DL), jnp.concatenate([hot_more, jnp.zeros_like(hot_more)], axis=1))

    settled(keys_turn.at[pl.ds(1, N - 1)], t_ss, t_rs).wait_recv()
    for p in range(N):

        def put(k, values, p=p):
            extra[k, p, :, pl.ds(0, 128)] = values

        unpack(keys_turn[p], put)
    for k in range(PARTS):
        for j in range(2):
            settled(keys.at[k, pl.ds(1, 15) if j == 0 else pl.ds(16, 16)], k_ss.at[k], k_rs.at[k, j]).wait_recv()
            run = pl.ds(16 * j, 16)
            add(keys[k, run].reshape(512, DL), extra[k, run].reshape(512, 256))

    lat_out[...] = (acc[...] / total[...]).astype(jnp.bfloat16)
    for p in range(1, N):
        dst = behind(me, OFFSETS[p])
        pltpu.make_async_remote_copy(
            src_ref=lat_out.at[pl.ds(16 * p, 16)],
            dst_ref=lat_in.at[pl.ds(pl.multiple_of(me * 16, 16), 16)],
            send_sem=o_ss, recv_sem=o_rs, **to(dst)
        ).start()
    lat_in[own, :] = lat_out[pl.ds(0, 16), :]
    settled(lat_in.at[pl.ds(0, 496)], o_ss, o_rs).wait_recv()
    loads[3].wait()
    got = lat_in[...]
    result = jnp.zeros((512, 128), jnp.float32)
    for h in range(4):
        result = jnp.where(row % 4 == h, jnp.dot(got, absorb_v[h], preferred_element_type=jnp.float32), result)
    out[...] = result.astype(jnp.bfloat16)

    settled(ids_in.at[pl.ds(1, N - 1)], ids_ss, ids_rs).wait_send()
    settled(q_out.at[pl.ds(0, 496)], q_ss, q_rs).wait_send()
    settled(stage_turn.at[pl.ds(1, N - 1)], t_ss, t_rs).wait_send()
    for k in range(PARTS):
        settled(stage.at[k, pl.ds(1, N - 1)], k_ss.at[k], k_rs.at[k, 0]).wait_send()
    settled(lat_out.at[pl.ds(0, 496)], o_ss, o_rs).wait_send()

    @pl.when(me == N - 1)
    def _():
        for copy in across:
            copy.wait_send()

    @pl.when((y == 3) & (c == 1))
    def _():
        for copy in down:
            copy.wait_send()

    @pl.when(c == 1)
    def _():
        for copy in over:
            copy.wait_send()


def body(query, absorb_k, absorb_v, latent_cache, cold_blocks):
    vmem = pl.BlockSpec(memory_space=pltpu.VMEM)
    bf16, f32, i32 = jnp.bfloat16, jnp.float32, jnp.int32
    dma = pltpu.SemaphoreType.DMA
    out = pl.pallas_call(
        kernel,
        out_shape=jax.ShapeDtypeStruct((512, 128), bf16),
        in_specs=[pl.BlockSpec(memory_space=pl.ANY)] * 4 + [vmem],
        out_specs=vmem,
        scratch_shapes=[
            pltpu.VMEM((4, 192, 128), bf16),
            pltpu.VMEM((512, DL), bf16),
            pltpu.VMEM((4, DL, 128), bf16),
            pltpu.VMEM((576, 1024), bf16),
            pltpu.VMEM((16, BLK, DL), bf16),
            pltpu.VMEM((16, BLK, 128), bf16),
            pltpu.VMEM((N, 1, 128), i32),
            pltpu.VMEM((N, 1, 128), i32),
            pltpu.SMEM((N, 1, 128), i32),
            pltpu.VMEM((2, N, 128), f32),
            pltpu.VMEM((512, 640), bf16),
            pltpu.VMEM((512, 768), bf16),
            pltpu.VMEM((PARTS, N, QUARTER, DL), bf16),
            pltpu.VMEM((N, 16, DL), bf16),
            pltpu.VMEM((PARTS, N, QUARTER, DL), bf16),
            pltpu.VMEM((N, 16, DL), bf16),
            pltpu.VMEM((PARTS, QUARTER, DL), bf16),
            pltpu.VMEM((16, DL), bf16),
            pltpu.VMEM((PARTS, N, QUARTER, 256), bf16),
            pltpu.VMEM((512, 1), f32),
            pltpu.VMEM((512, 1), f32),
            pltpu.VMEM((512, DL), f32),
            pltpu.VMEM((512, DL), bf16),
            pltpu.VMEM((512, DL), bf16),
        ]
        + [dma, dma, dma, dma, dma((PARTS,)), dma((PARTS, 2)), dma, dma, dma, dma]
        + [dma((2, 7)), dma((2,)), dma, dma((4,))],
        compiler_params=pltpu.CompilerParams(collective_id=0, has_side_effects=True, vmem_limit_bytes=64 * 2**20 - 160 * 2**10),
    )(
        query.transpose(1, 2, 0),
        absorb_k.reshape(512, DL),
        absorb_v,
        latent_cache.T,
        cold_blocks,
    )
    return out.reshape(128, 4, 128)


def solution(mesh):
    placed = (
        P("grp", "ctx", None),
        P("ctx", None, None),
        P("ctx", None, None),
        P("ctx", None),
        P(("grp", "ctx"), None),
    )
    return jax.shard_map(
        body, mesh=mesh, in_specs=placed, out_specs=P("grp", "ctx", None), check_vma=False
    )
```

```python
import functools
import math

import jax
import jax.numpy as jnp
from jax import lax
from jax.experimental import pallas as pl
from jax.experimental.pallas import tpu as pltpu
from jax.sharding import PartitionSpec as P

MESH = pl.DeviceIdType.MESH
DL = 512
DN = 128
BLK = 64
N = 32
NEG = -1e30

AXIS = (0, 3, 1, 2)
SERVED = ((0, 1), (0, 3), (0, 2), (1, 1), (1, 3), (1, 2), (1, 0))

RINGS = (
    ((1, 1), (3, 3), (1, 3), (3, 1)),
    ((2, 1), (0, 1), (2, 3), (0, 3)),
    ((2, 2),),
    ((1, 2), (1, 0), (3, 2), (3, 0)),
    ((2, 0), (0, 2)),
)
OFFSETS = [(0, 0, 0)]
for ring in RINGS:
    for core in (0, 1):
        OFFSETS += [(dx, dy, core) for dx, dy in ring]
OFFSETS.append((0, 0, 1))


def ahead(me, offset):
    dx, dy, dc = offset
    x, y, c = me // 8, (me // 2) % 4, me % 2
    return (((x + dx) % 4) * 4 + (y + dy) % 4) * 2 + (c + dc) % 2


def behind(me, offset):
    dx, dy, dc = offset
    return ahead(me, ((4 - dx) % 4, (4 - dy) % 4, dc))


def to(device):
    return dict(device_id={"ctx": device}, device_id_type=MESH)


def pack(rows, rope, id0, id1, first, second, turns):
    first[...] = rows[id0]
    second[...] = rows[id1]
    lane = lax.broadcasted_iota(jnp.int32, (BLK, 128), 1)
    both = jnp.where(lane < 64, rope[id0], rope[id1])
    for b in range(4):
        turns[:, pl.ds(128 * b, 128)] = both[16 * b : 16 * b + 16]


def kernel(
    query_at, absorb_k_at, absorb_v_at, stored_at, cold, out,
    query, absorb_k, absorb_v, stored,
    rows0, rows1, rows2, rows3, rope, pairs, ids_out, ids_in, ids, bias, q_out, q_all, stage, stage_turn, keys, keys_turn, hot, hot_turn, extra,
    top, total, acc, lat_out, lat_in,
    ids_ss, ids_rs, own_ss, own_rs, fwd_ss, fwd_rs, q_ss, q_rs, k_ss, k_rs, t_ss, t_rs, o_ss, o_rs, hot_ss, hot_rs, id_sem, in_sem,
):
    me = lax.axis_index("ctx")
    x, y, c = me // 8, (me // 2) % 4, me % 2

    def place(core):
        return jnp.where(core == 0, y, x), jnp.where(core == 0, x, y)

    def device(core, u, v):
        return (jnp.where(core == 0, v, u) * 4 + jnp.where(core == 0, u, v)) * 2 + core

    u, v = place(c)
    rows = (rows0, rows1, rows2, rows3)
    plus, minus = device(c, u, (v + 1) % 4), device(c, u, (v + 3) % 4)

    def served(flip, e):
        return device(c, (u + e) % 4, v) - c + (c + flip) % 2

    def server(flip, e):
        core = (c + flip) % 2
        cu, cv = place(core)
        return device(core, (cu + 4 - e) % 4, cv), core * 16 + (cu + 4 - e) % 4 * 4, cv

    barrier = pltpu.get_barrier_semaphore()
    for p in range(1, N):
        pl.semaphore_signal(barrier, inc=1, **to(ahead(me, OFFSETS[p])))

    loads = [
        pltpu.make_async_copy(src, dst, in_sem.at[k])
        for k, (src, dst) in enumerate(
            ((stored_at, stored), (query_at, query), (absorb_k_at, absorb_k), (absorb_v_at, absorb_v))
        )
    ]
    for load in loads:
        load.start()

    line = lax.broadcasted_iota(jnp.int32, (N, 1), 0)
    core, cu, cv = line // 16, (line // 4) % 4, line % 4
    base = jnp.where(core == 0, cv * 8 + cu * 2, cu * 8 + cv * 2 + 1) * 16
    local = [cold[r : r + 1, :] - base for r in range(4)]
    low, high = None, None
    for r in range(4):
        inside = (local[r] >= 0) & (local[r] < 16)
        a = jnp.min(jnp.where(inside, local[r], 99), axis=1, keepdims=True)
        b = jnp.max(jnp.where(inside, local[r], -1), axis=1, keepdims=True)
        low = a if r == 0 else jnp.minimum(low, a)
        high = b if r == 0 else jnp.maximum(high, b)
    id0 = jnp.where(high < 0, 0, low)
    id1 = jnp.where(high < 0, 0, high)
    lane = lax.broadcasted_iota(jnp.int32, (N, 128), 1)
    ids_out[...] = jnp.where(lane == 0, id0, id1).reshape(N, 1, 128)
    for s, wanted in ((0, id0), (1, id1)):
        mark = jnp.zeros((N, 128), jnp.float32)
        for r in range(4):
            found = jnp.max(jnp.where(local[r] == wanted, 1, 0), axis=1, keepdims=True)
            if s == 1:
                found = jnp.where(id1 == id0, 0, found)
            mark = jnp.where((lane == r) & (found == 0), NEG, mark)
        bias[s] = mark

    lanes = (((1,), (1,)), ((), ()))
    unit = jnp.where(
        lax.broadcasted_iota(jnp.int32, (256, 256), 0) == lax.broadcasted_iota(jnp.int32, (256, 256), 1), 1.0, 0.0
    ).astype(jnp.bfloat16)
    loads[0].wait()
    for k in range(4):
        part = pl.ds(256 * k, 256)
        turned = lax.dot_general(unit, stored[:DL, part], lanes, preferred_element_type=jnp.float32)
        rows[0][pl.ds(4 * k, 4)] = turned.astype(jnp.bfloat16).reshape(4, BLK, DL)
        tail = stored[DL:, part]
        turned = lax.dot_general(
            unit, jnp.concatenate([tail, tail], axis=0), lanes, preferred_element_type=jnp.float32
        )
        rope[0, pl.ds(4 * k, 4)] = turned.astype(jnp.bfloat16).reshape(4, BLK, 128)
    low_lanes = lax.broadcasted_iota(jnp.int32, (8, BLK, 128), 2) < 64
    pairs[0] = jnp.where(low_lanes, rope[0, pl.ds(0, 8)], rope[0, pl.ds(8, 8)])

    pl.semaphore_wait(barrier, N - 1)
    for flip, e in SERVED:
        there, first_row, _ = server(flip, e)
        pltpu.make_async_remote_copy(
            src_ref=ids_out.at[pl.ds(first_row, 4)], dst_ref=ids_in.at[4 * flip + e],
            send_sem=ids_ss, recv_sem=ids_rs, **to(there)
        ).start()
    ids_in[0] = ids_out[pl.ds(c * 16 + u * 4, 4)]

    def settled(ref, sends, lands):
        return pltpu.make_async_remote_copy(src_ref=ref, dst_ref=ref, send_sem=sends, recv_sem=lands, **to(ahead(me, OFFSETS[1])))

    def hot_copies(k, offset):
        device = to(ahead(me, offset))
        return [
            pltpu.make_async_remote_copy(
                src_ref=ref, dst_ref=ref, send_sem=hot_ss.at[i, k], recv_sem=hot_rs.at[i], **device
            )
            for i, ref in enumerate((hot, hot_turn))
        ]

    across = hot_copies(0, (1, 0, 0)) + hot_copies(1, (2, 0, 0)) + hot_copies(2, (3, 0, 0))
    down = hot_copies(3, (0, 1, 0)) + hot_copies(4, (0, 2, 0)) + hot_copies(5, (0, 3, 0))
    over = hot_copies(6, (0, 0, 1))

    @pl.when(me == N - 1)
    def _():
        pack(rows[0], rope.at[0], 14, 15, hot.at[0], hot.at[1], hot_turn)
        for copy in across + down:
            copy.start()

    def hop(src, dst, half, there, sends, lands):
        span, turns = pl.ds(8 * half, 8), pl.ds(4 * half, 4)
        return [
            pltpu.make_async_remote_copy(
                src_ref=a, dst_ref=b, send_sem=sends.at[i], recv_sem=lands.at[i], **to(there)
            )
            for i, (a, b) in enumerate(
                ((rows[src].at[span], rows[dst].at[span]), (pairs.at[src, turns], pairs.at[dst, turns]))
            )
        ]

    own_up = [hop(0, 1, h, plus, own_ss.at[0, h], own_rs.at[0, h]) for h in (0, 1)]
    own_down = [hop(0, 2, h, minus, own_ss.at[1, h], own_rs.at[1, h]) for h in (0, 1)]
    on_up = hop(1, 3, 0, plus, fwd_ss.at[0], fwd_rs.at[0])
    on_down = hop(2, 3, 1, minus, fwd_ss.at[1], fwd_rs.at[1])

    def start(*groups):
        for copies in groups:
            for copy in copies:
                copy.start()

    def arrive(*groups):
        for copies in groups:
            for copy in copies:
                copy.wait_recv()

    start(own_up[0], own_down[1])

    row = lax.broadcasted_iota(jnp.int32, (512, 128), 0)
    column = lax.broadcasted_iota(jnp.int32, (512, 128), 1)
    plain, turn = [], None
    loads[1].wait()
    loads[2].wait()
    for h in range(4):
        pick = jnp.where(row == 4 * column + h, 1.0, 0.0).astype(jnp.bfloat16)
        spread = lax.dot_general(pick, query[h], lanes, preferred_element_type=jnp.float32)
        plain.append(spread[:, :DN].astype(jnp.bfloat16))
        turn = spread[:, DN:] if h == 0 else turn + spread[:, DN:]
    q_out[:, :DL] = jnp.dot(
        jnp.concatenate(plain, axis=1), absorb_k[...], preferred_element_type=jnp.float32
    ).astype(jnp.bfloat16)
    turn = turn.astype(jnp.bfloat16)
    q_out[:, DL:] = jnp.concatenate([turn, turn], axis=1)
    for p in range(1, N):
        dst = ahead(me, OFFSETS[p])
        pltpu.make_async_remote_copy(
            src_ref=q_out.at[pl.ds(pl.multiple_of(dst * 16, 16), 16)],
            dst_ref=q_all.at[pl.ds(16 * p, 16), pl.ds(0, 640)],
            send_sem=q_ss, recv_sem=q_rs, **to(dst)
        ).start()

    @pl.when((y == 3) & (c == 1) & (x != 3))
    def _():
        arrive(across[:2])
        start(down)

    start(own_up[1], own_down[0])

    settled(ids_in.at[pl.ds(1, 7)], ids_ss, ids_rs).wait_recv()
    fetch = pltpu.make_async_copy(ids_in, ids, id_sem)
    fetch.start()
    fetch.wait()

    def serve(w):
        at = (v + AXIS[w]) % 4
        for flip, e in SERVED:
            j = 4 * flip + e
            pack(
                rows[w], rope.at[w], ids[j, at, 0, 0], ids[j, at, 0, 1],
                stage.at[w, 0, j], stage.at[w, 1, j], stage_turn.at[w, j]
            )
            there = to(served(flip, e))
            pltpu.make_async_remote_copy(
                src_ref=stage_turn.at[w, j], dst_ref=keys_turn.at[w, j],
                send_sem=t_ss.at[w], recv_sem=t_rs.at[w], **there
            ).start()
            pltpu.make_async_remote_copy(
                src_ref=stage.at[w, 0, j], dst_ref=keys.at[w, 0, j],
                send_sem=k_ss.at[w, 0], recv_sem=k_rs.at[w, 0], **there
            ).start()
        for flip, e in SERVED:
            j = 4 * flip + e
            pltpu.make_async_remote_copy(
                src_ref=stage.at[w, 1, j], dst_ref=keys.at[w, 1, j],
                send_sem=k_ss.at[w, 1], recv_sem=k_rs.at[w, 1], **to(served(flip, e))
            ).start()
        pack(
            rows[w], rope.at[w], ids[0, at, 0, 0], ids[0, at, 0, 1],
            keys.at[w, 0, 0], keys.at[w, 1, 0], keys_turn.at[w, 0]
        )

    def widen(w):
        both = pairs[w]
        for half in (0, 1):
            one = both[:, :, 64 * half : 64 * half + 64]
            rope[w, pl.ds(8 * half, 8)] = jnp.concatenate([one, one], axis=2)

    serve(0)
    arrive(own_up[0], own_down[1])
    start(on_up, on_down)

    own = pl.ds(pl.multiple_of(me * 16, 16), 16)
    q_all[pl.ds(0, 16), pl.ds(0, 640)] = q_out[own, :]
    marks = (lax.broadcasted_iota(jnp.int32, (512, 128), 0) // 4) % 4 == lax.broadcasted_iota(
        jnp.int32, (512, 128), 1
    )
    q_all[:, 640:] = jnp.where(marks, 1.0, 0.0).astype(jnp.bfloat16)
    for flip in (0, 1):
        for e in range(4):
            _, first_row, at = server(flip, e)
            for w in range(4):
                for i in (0, 1):
                    mark = bias[i, pl.ds(first_row + (at + AXIS[w]) % 4, 1), :]
                    extra[w, i, 4 * flip + e, :, pl.ds(128, 128)] = jnp.broadcast_to(mark, (BLK, 128)).astype(
                        jnp.bfloat16
                    )
    arrive(own_up[1])
    widen(1)

    @pl.when((c == 1) & (y != 3))
    def _():
        arrive(down[:2])

    @pl.when(c == 1)
    def _():
        start(over)

    serve(1)
    arrive(own_down[0])
    widen(2)
    serve(2)
    settled(q_all.at[pl.ds(16, 496), pl.ds(0, 640)], q_ss, q_rs).wait_recv()

    scale = math.log2(math.e) / math.sqrt(192)
    first = lax.broadcasted_iota(jnp.int32, (BLK, 128), 1) < 64
    none = jnp.zeros((BLK, 128), jnp.bfloat16)

    def unpack(turns):
        both = jnp.concatenate([turns[:, 128 * b : 128 * b + 128] for b in range(4)], axis=0)
        return jnp.where(first, both, none), jnp.where(first, none, both)

    def scores(latent, more):
        s = lax.dot_general(q_all[:, :DL], latent, lanes, preferred_element_type=jnp.float32)
        s += lax.dot_general(q_all[:, DL:], more, lanes, preferred_element_type=jnp.float32)
        return s * scale

    def add(latent, more):
        s = scores(latent, more)
        old = top[...]
        new = jnp.maximum(old, jnp.max(s, axis=1, keepdims=True))
        fade = jnp.exp2(old - new)
        w = jnp.exp2(s - new)
        total[...] = total[...] * fade + jnp.sum(w, axis=1, keepdims=True)
        top[...] = new
        acc[...] = acc[...] * fade + jnp.dot(
            w.astype(jnp.bfloat16), latent, preferred_element_type=jnp.float32
        )

    top[...] = jnp.full((512, 1), NEG, jnp.float32)
    total[...] = jnp.zeros((512, 1), jnp.float32)
    acc[...] = jnp.zeros((512, DL), jnp.float32)

    def attend(w):
        settled(keys_turn.at[w, pl.ds(1, 7)], t_ss.at[w], t_rs.at[w]).wait_recv()
        for j in range(8):
            for i, values in enumerate(unpack(keys_turn[w, j])):
                extra[w, i, j, :, pl.ds(0, 128)] = values
        for i in (0, 1):
            settled(keys.at[w, i, pl.ds(1, 7)], k_ss.at[w, i], k_rs.at[w, i]).wait_recv()
            add(keys[w, i].reshape(512, DL), extra[w, i].reshape(512, 256))

    attend(0)
    arrive(on_up, on_down)
    widen(3)
    serve(3)

    @pl.when(c == 0)
    def _():
        arrive(over)

    hot_more = jnp.concatenate(unpack(hot_turn[...]), axis=0)
    add(hot[...].reshape(128, DL), jnp.concatenate([hot_more, jnp.zeros_like(hot_more)], axis=1))
    for w in (1, 2, 3):
        attend(w)

    lat_out[...] = (acc[...] / total[...]).astype(jnp.bfloat16)
    for p in range(1, N):
        dst = behind(me, OFFSETS[p])
        pltpu.make_async_remote_copy(
            src_ref=lat_out.at[pl.ds(16 * p, 16)],
            dst_ref=lat_in.at[pl.ds(pl.multiple_of(me * 16, 16), 16)],
            send_sem=o_ss, recv_sem=o_rs, **to(dst)
        ).start()
    lat_in[own, :] = lat_out[pl.ds(0, 16), :]
    settled(lat_in.at[pl.ds(0, 496)], o_ss, o_rs).wait_recv()
    loads[3].wait()
    got = lat_in[...]
    result = jnp.zeros((512, 128), jnp.float32)
    for h in range(4):
        result = jnp.where(row % 4 == h, jnp.dot(got, absorb_v[h], preferred_element_type=jnp.float32), result)
    out[...] = result.astype(jnp.bfloat16)

    settled(ids_in.at[pl.ds(1, 7)], ids_ss, ids_rs).wait_send()
    settled(q_out.at[pl.ds(0, 496)], q_ss, q_rs).wait_send()
    for copy in own_up[0] + own_up[1] + own_down[0] + own_down[1] + on_up + on_down:
        copy.wait_send()
    for w in range(4):
        settled(stage_turn.at[w, pl.ds(1, 7)], t_ss.at[w], t_rs.at[w]).wait_send()
        for i in (0, 1):
            settled(stage.at[w, i, pl.ds(1, 7)], k_ss.at[w, i], k_rs.at[w, i]).wait_send()
    settled(lat_out.at[pl.ds(0, 496)], o_ss, o_rs).wait_send()

    @pl.when(me == N - 1)
    def _():
        for copy in across:
            copy.wait_send()

    @pl.when((y == 3) & (c == 1))
    def _():
        for copy in down:
            copy.wait_send()

    @pl.when(c == 1)
    def _():
        for copy in over:
            copy.wait_send()


def body(query, absorb_k, absorb_v, latent_cache, cold_blocks):
    vmem = pl.BlockSpec(memory_space=pltpu.VMEM)
    bf16, f32, i32 = jnp.bfloat16, jnp.float32, jnp.int32
    dma = pltpu.SemaphoreType.DMA
    out = pl.pallas_call(
        kernel,
        out_shape=jax.ShapeDtypeStruct((512, 128), bf16),
        in_specs=[pl.BlockSpec(memory_space=pl.ANY)] * 4 + [vmem],
        out_specs=vmem,
        scratch_shapes=[
            pltpu.VMEM((4, 192, 128), bf16),
            pltpu.VMEM((512, DL), bf16),
            pltpu.VMEM((4, DL, 128), bf16),
            pltpu.VMEM((576, 1024), bf16),
            pltpu.VMEM((16, BLK, DL), bf16),
            pltpu.VMEM((16, BLK, DL), bf16),
            pltpu.VMEM((16, BLK, DL), bf16),
            pltpu.VMEM((16, BLK, DL), bf16),
            pltpu.VMEM((4, 16, BLK, 128), bf16),
            pltpu.VMEM((4, 8, BLK, 128), bf16),
            pltpu.VMEM((N, 1, 128), i32),
            pltpu.VMEM((8, 4, 1, 128), i32),
            pltpu.SMEM((8, 4, 1, 128), i32),
            pltpu.VMEM((2, N, 128), f32),
            pltpu.VMEM((512, 640), bf16),
            pltpu.VMEM((512, 768), bf16),
            pltpu.VMEM((4, 2, 8, BLK, DL), bf16),
            pltpu.VMEM((4, 8, 16, DL), bf16),
            pltpu.VMEM((4, 2, 8, BLK, DL), bf16),
            pltpu.VMEM((4, 8, 16, DL), bf16),
            pltpu.VMEM((2, BLK, DL), bf16),
            pltpu.VMEM((16, DL), bf16),
            pltpu.VMEM((4, 2, 8, BLK, 256), bf16),
            pltpu.VMEM((512, 1), f32),
            pltpu.VMEM((512, 1), f32),
            pltpu.VMEM((512, DL), f32),
            pltpu.VMEM((512, DL), bf16),
            pltpu.VMEM((512, DL), bf16),
        ]
        + [dma, dma, dma((2, 2, 2)), dma((2, 2, 2)), dma((2, 2)), dma((2, 2)), dma, dma]
        + [dma((4, 2)), dma((4, 2)), dma((4,)), dma((4,)), dma, dma]
        + [dma((2, 7)), dma((2,)), dma, dma((4,))],
        compiler_params=pltpu.CompilerParams(collective_id=0, has_side_effects=True, vmem_limit_bytes=64 * 2**20 - 160 * 2**10),
    )(
        query.transpose(1, 2, 0),
        absorb_k.reshape(512, DL),
        absorb_v,
        latent_cache.T,
        cold_blocks,
    )
    return out.reshape(128, 4, 128)


def solution(mesh):
    placed = (
        P("grp", "ctx", None),
        P("ctx", None, None),
        P("ctx", None, None),
        P("ctx", None),
        P(("grp", "ctx"), None),
    )
    return jax.shard_map(
        body, mesh=mesh, in_specs=placed, out_specs=P("grp", "ctx", None), check_vma=False
    )
```

```python
import functools
import math

import jax
import jax.numpy as jnp
from jax import lax
from jax.experimental import pallas as pl
from jax.experimental.pallas import tpu as pltpu
from jax.sharding import PartitionSpec as P

MESH = pl.DeviceIdType.MESH
DL = 512
DN = 128
BLK = 64
N = 32
NEG = -1e30

AXIS = (0, 3, 1, 2)
SERVED = ((0, 1), (0, 3), (0, 2), (1, 1), (1, 3), (1, 2), (1, 0))

RINGS = (
    ((2, 2),),
    ((2, 1), (1, 2), (2, 3), (3, 2)),
    ((1, 1), (3, 3), (1, 3), (3, 1)),
    ((2, 0), (0, 2)),
    ((1, 0), (0, 1), (3, 0), (0, 3)),
)
OFFSETS = [(0, 0, 0)]
for ring in RINGS:
    for core in (0, 1):
        OFFSETS += [(dx, dy, core) for dx, dy in ring]
OFFSETS.append((0, 0, 1))


def ahead(me, offset):
    dx, dy, dc = offset
    x, y, c = me // 8, (me // 2) % 4, me % 2
    return (((x + dx) % 4) * 4 + (y + dy) % 4) * 2 + (c + dc) % 2


def behind(me, offset):
    dx, dy, dc = offset
    return ahead(me, ((4 - dx) % 4, (4 - dy) % 4, dc))


def to(device):
    return dict(device_id={"ctx": device}, device_id_type=MESH)


def pack(rows, rope, id0, id1, first, second, turns):
    first[...] = rows[id0]
    second[...] = rows[id1]
    lane = lax.broadcasted_iota(jnp.int32, (BLK, 128), 1)
    both = jnp.where(lane < 64, rope[id0], rope[id1])
    for b in range(4):
        turns[:, pl.ds(128 * b, 128)] = both[16 * b : 16 * b + 16]


def kernel(
    query_at, absorb_k_at, absorb_v_at, stored_at, cold, out,
    query, absorb_k, absorb_v, stored,
    rows0, rows1, rows2, rows3, rope, pairs, ids_out, ids_in, ids, bias, q_out, q_all, stage, stage_turn, keys, keys_turn, hot, hot_turn, extra,
    top, total, acc, lat_out, lat_in,
    ids_ss, ids_rs, own_ss, own_rs, fwd_ss, fwd_rs, q_ss, q_rs, k_ss, k_rs, t_ss, t_rs, o_ss, o_rs, hot_ss, hot_rs, id_sem, in_sem, all_in,
):
    me = lax.axis_index("ctx")
    x, y, c = me // 8, (me // 2) % 4, me % 2

    def place(core):
        return jnp.where(core == 0, y, x), jnp.where(core == 0, x, y)

    def device(core, u, v):
        return (jnp.where(core == 0, v, u) * 4 + jnp.where(core == 0, u, v)) * 2 + core

    u, v = place(c)
    rows = (rows0, rows1, rows2, rows3)
    plus, minus = device(c, u, (v + 1) % 4), device(c, u, (v + 3) % 4)

    def served(flip, e):
        return device(c, (u + e) % 4, v) - c + (c + flip) % 2

    def server(flip, e):
        core = (c + flip) % 2
        cu, cv = place(core)
        return device(core, (cu + 4 - e) % 4, cv), core * 16 + (cu + 4 - e) % 4 * 4, cv

    barrier = pltpu.get_barrier_semaphore()
    crossing = [offset for offset in OFFSETS[1:] if 0 in offset[:2]]
    for offset in crossing:
        pl.semaphore_signal(barrier, inc=1, **to(ahead(me, offset)))

    loads = [
        pltpu.make_async_copy(src, dst, in_sem.at[k])
        for k, (src, dst) in enumerate(
            ((stored_at, stored), (query_at, query), (absorb_k_at, absorb_k), (absorb_v_at, absorb_v))
        )
    ]
    for load in loads:
        load.start()

    line = lax.broadcasted_iota(jnp.int32, (N, 1), 0)
    core, cu, cv = line // 16, (line // 4) % 4, line % 4
    base = jnp.where(core == 0, cv * 8 + cu * 2, cu * 8 + cv * 2 + 1) * 16
    local = [cold[r : r + 1, :] - base for r in range(4)]
    low, high = None, None
    for r in range(4):
        inside = (local[r] >= 0) & (local[r] < 16)
        a = jnp.min(jnp.where(inside, local[r], 99), axis=1, keepdims=True)
        b = jnp.max(jnp.where(inside, local[r], -1), axis=1, keepdims=True)
        low = a if r == 0 else jnp.minimum(low, a)
        high = b if r == 0 else jnp.maximum(high, b)
    id0 = jnp.where(high < 0, 0, low)
    id1 = jnp.where(high < 0, 0, high)
    lane = lax.broadcasted_iota(jnp.int32, (N, 128), 1)
    ids_out[...] = jnp.where(lane == 0, id0, id1).reshape(N, 1, 128)
    for s, wanted in ((0, id0), (1, id1)):
        mark = jnp.zeros((N, 128), jnp.float32)
        for r in range(4):
            found = jnp.max(jnp.where(local[r] == wanted, 1, 0), axis=1, keepdims=True)
            if s == 1:
                found = jnp.where(id1 == id0, 0, found)
            mark = jnp.where((lane == r) & (found == 0), NEG, mark)
        bias[s] = mark

    lanes = (((1,), (1,)), ((), ()))
    unit = jnp.where(
        lax.broadcasted_iota(jnp.int32, (256, 256), 0) == lax.broadcasted_iota(jnp.int32, (256, 256), 1), 1.0, 0.0
    ).astype(jnp.bfloat16)
    loads[0].wait()
    for k in range(4):
        part = pl.ds(256 * k, 256)
        turned = lax.dot_general(unit, stored[:DL, part], lanes, preferred_element_type=jnp.float32)
        rows[0][pl.ds(4 * k, 4)] = turned.astype(jnp.bfloat16).reshape(4, BLK, DL)
        tail = stored[DL:, part]
        turned = lax.dot_general(
            unit, jnp.concatenate([tail, tail], axis=0), lanes, preferred_element_type=jnp.float32
        )
        rope[0, pl.ds(4 * k, 4)] = turned.astype(jnp.bfloat16).reshape(4, BLK, 128)
    low_lanes = lax.broadcasted_iota(jnp.int32, (8, BLK, 128), 2) < 64
    pairs[0] = jnp.where(low_lanes, rope[0, pl.ds(0, 8)], rope[0, pl.ds(8, 8)])

    pl.semaphore_wait(barrier, len(crossing))
    for offset in crossing:
        pl.semaphore_signal(all_in, inc=1, **to(ahead(me, offset)))
    for flip, e in SERVED:
        there, first_row, _ = server(flip, e)
        pltpu.make_async_remote_copy(
            src_ref=ids_out.at[pl.ds(first_row, 4)], dst_ref=ids_in.at[4 * flip + e],
            send_sem=ids_ss, recv_sem=ids_rs, **to(there)
        ).start()
    ids_in[0] = ids_out[pl.ds(c * 16 + u * 4, 4)]

    def settled(ref, sends, lands):
        return pltpu.make_async_remote_copy(src_ref=ref, dst_ref=ref, send_sem=sends, recv_sem=lands, **to(ahead(me, OFFSETS[1])))

    def hot_copies(k, offset):
        device = to(ahead(me, offset))
        return [
            pltpu.make_async_remote_copy(
                src_ref=ref, dst_ref=ref, send_sem=hot_ss.at[i, k], recv_sem=hot_rs.at[i], **device
            )
            for i, ref in enumerate((hot, hot_turn))
        ]

    across = hot_copies(0, (1, 0, 0)) + hot_copies(1, (2, 0, 0)) + hot_copies(2, (3, 0, 0))
    down = hot_copies(3, (0, 1, 0)) + hot_copies(4, (0, 2, 0)) + hot_copies(5, (0, 3, 0))
    over = hot_copies(6, (0, 0, 1))

    @pl.when(me == N - 1)
    def _():
        pack(rows[0], rope.at[0], 14, 15, hot.at[0], hot.at[1], hot_turn)
        for copy in across + down:
            copy.start()

    def hop(src, dst, half, there, sends, lands):
        span, turns = pl.ds(8 * half, 8), pl.ds(4 * half, 4)
        return [
            pltpu.make_async_remote_copy(
                src_ref=a, dst_ref=b, send_sem=sends.at[i], recv_sem=lands.at[i], **to(there)
            )
            for i, (a, b) in enumerate(
                ((rows[src].at[span], rows[dst].at[span]), (pairs.at[src, turns], pairs.at[dst, turns]))
            )
        ]

    own_up = [hop(0, 1, h, plus, own_ss.at[0, h], own_rs.at[0, h]) for h in (0, 1)]
    own_down = [hop(0, 2, h, minus, own_ss.at[1, h], own_rs.at[1, h]) for h in (0, 1)]
    on_up = hop(1, 3, 0, plus, fwd_ss.at[0], fwd_rs.at[0])
    on_down = hop(2, 3, 1, minus, fwd_ss.at[1], fwd_rs.at[1])

    def start(*groups):
        for copies in groups:
            for copy in copies:
                copy.start()

    def arrive(*groups):
        for copies in groups:
            for copy in copies:
                copy.wait_recv()

    start(own_up[0], own_down[1])

    row = lax.broadcasted_iota(jnp.int32, (512, 128), 0)
    column = lax.broadcasted_iota(jnp.int32, (512, 128), 1)
    plain, turn = [], None
    loads[1].wait()
    loads[2].wait()
    for h in range(4):
        pick = jnp.where(row == 4 * column + h, 1.0, 0.0).astype(jnp.bfloat16)
        spread = lax.dot_general(pick, query[h], lanes, preferred_element_type=jnp.float32)
        plain.append(spread[:, :DN].astype(jnp.bfloat16))
        turn = spread[:, DN:] if h == 0 else turn + spread[:, DN:]
    q_out[:, :DL] = jnp.dot(
        jnp.concatenate(plain, axis=1), absorb_k[...], preferred_element_type=jnp.float32
    ).astype(jnp.bfloat16)
    turn = turn.astype(jnp.bfloat16)
    q_out[:, DL:] = jnp.concatenate([turn, turn], axis=1)
    pl.semaphore_wait(all_in, len(crossing))
    for p in range(1, N):
        dst = ahead(me, OFFSETS[p])
        pltpu.make_async_remote_copy(
            src_ref=q_out.at[pl.ds(pl.multiple_of(dst * 16, 16), 16)],
            dst_ref=q_all.at[pl.ds(16 * p, 16), pl.ds(0, 640)],
            send_sem=q_ss, recv_sem=q_rs, **to(dst)
        ).start()

    @pl.when((y == 3) & (c == 1) & (x != 3))
    def _():
        arrive(across[:2])
        start(down)

    start(own_up[1], own_down[0])

    settled(ids_in.at[pl.ds(1, 7)], ids_ss, ids_rs).wait_recv()
    fetch = pltpu.make_async_copy(ids_in, ids, id_sem)
    fetch.start()
    fetch.wait()

    def serve(w):
        at = (v + AXIS[w]) % 4
        for flip, e in SERVED:
            j = 4 * flip + e
            pack(
                rows[w], rope.at[w], ids[j, at, 0, 0], ids[j, at, 0, 1],
                stage.at[w, 0, j], stage.at[w, 1, j], stage_turn.at[w, j]
            )
            there = to(served(flip, e))
            pltpu.make_async_remote_copy(
                src_ref=stage_turn.at[w, j], dst_ref=keys_turn.at[w, j],
                send_sem=t_ss.at[w], recv_sem=t_rs.at[w], **there
            ).start()
            pltpu.make_async_remote_copy(
                src_ref=stage.at[w, 0, j], dst_ref=keys.at[w, 0, j],
                send_sem=k_ss.at[w, 0], recv_sem=k_rs.at[w, 0], **there
            ).start()
        for flip, e in SERVED:
            j = 4 * flip + e
            pltpu.make_async_remote_copy(
                src_ref=stage.at[w, 1, j], dst_ref=keys.at[w, 1, j],
                send_sem=k_ss.at[w, 1], recv_sem=k_rs.at[w, 1 + flip], **to(served(flip, e))
            ).start()
        pack(
            rows[w], rope.at[w], ids[0, at, 0, 0], ids[0, at, 0, 1],
            keys.at[w, 0, 0], keys.at[w, 1, 0], keys_turn.at[w, 0]
        )

    def widen(w):
        both = pairs[w]
        for half in (0, 1):
            one = both[:, :, 64 * half : 64 * half + 64]
            rope[w, pl.ds(8 * half, 8)] = jnp.concatenate([one, one], axis=2)

    serve(0)
    arrive(own_up[0], own_down[1])
    start(on_up, on_down)

    own = pl.ds(pl.multiple_of(me * 16, 16), 16)
    q_all[pl.ds(0, 16), pl.ds(0, 640)] = q_out[own, :]
    marks = (lax.broadcasted_iota(jnp.int32, (512, 128), 0) // 4) % 4 == lax.broadcasted_iota(
        jnp.int32, (512, 128), 1
    )
    q_all[:, 640:] = jnp.where(marks, 1.0, 0.0).astype(jnp.bfloat16)
    for flip in (0, 1):
        for e in range(4):
            _, first_row, at = server(flip, e)
            for w in range(4):
                for i in (0, 1):
                    mark = bias[i, pl.ds(first_row + (at + AXIS[w]) % 4, 1), :]
                    extra[w, i, 4 * flip + e, :, pl.ds(128, 128)] = jnp.broadcast_to(mark, (BLK, 128)).astype(
                        jnp.bfloat16
                    )
    arrive(own_up[1])
    widen(1)

    @pl.when((c == 1) & (y != 3))
    def _():
        arrive(down[:2])

    @pl.when(c == 1)
    def _():
        start(over)

    serve(1)
    arrive(own_down[0])
    widen(2)
    serve(2)

    scale = math.log2(math.e) / math.sqrt(192)
    first = lax.broadcasted_iota(jnp.int32, (BLK, 128), 1) < 64
    none = jnp.zeros((BLK, 128), jnp.bfloat16)

    def unpack(turns):
        both = jnp.concatenate([turns[:, 128 * b : 128 * b + 128] for b in range(4)], axis=0)
        return jnp.where(first, both, none), jnp.where(first, none, both)

    def add(latent, more, part=slice(None)):
        s = lax.dot_general(q_all[part, :DL], latent, lanes, preferred_element_type=jnp.float32)
        s += lax.dot_general(q_all[part, DL:], more, lanes, preferred_element_type=jnp.float32)
        s *= scale
        old = top[part]
        new = jnp.maximum(old, jnp.max(s, axis=1, keepdims=True))
        fade = jnp.exp2(old - new)
        w = jnp.exp2(s - new)
        total[part] = total[part] * fade + jnp.sum(w, axis=1, keepdims=True)
        top[part] = new
        acc[part] = acc[part] * fade + jnp.dot(
            w.astype(jnp.bfloat16), latent, preferred_element_type=jnp.float32
        )

    top[...] = jnp.full((512, 1), NEG, jnp.float32)
    total[...] = jnp.zeros((512, 1), jnp.float32)
    acc[...] = jnp.zeros((512, DL), jnp.float32)

    def prepare(w):
        settled(keys_turn.at[w, pl.ds(1, 7)], t_ss.at[w], t_rs.at[w]).wait_recv()
        for j in range(8):
            for i, values in enumerate(unpack(keys_turn[w, j])):
                extra[w, i, j, :, pl.ds(0, 128)] = values

    def landed(w, i, flips=(0, 1)):
        for flip in flips if i else (0,):
            span = pl.ds(4 * flip + 1 - flip, 3 + flip) if i else pl.ds(1, 7)
            settled(keys.at[w, i, span], k_ss.at[w, i], k_rs.at[w, i + flip]).wait_recv()
        run = pl.ds(4 * flips[0], 4 * len(flips))
        tokens = 256 * len(flips)
        return keys[w, i, run].reshape(tokens, DL), extra[w, i, run].reshape(tokens, 256)

    def attend(w):
        prepare(w)
        for i in (0, 1):
            add(*landed(w, i))

    settled(q_all.at[pl.ds(16, 496), pl.ds(0, 640)], q_ss, q_rs).wait_recv()
    attend(0)
    arrive(on_up, on_down)
    widen(3)
    serve(3)

    @pl.when(c == 0)
    def _():
        arrive(over)

    hot_more = jnp.concatenate(unpack(hot_turn[...]), axis=0)
    add(hot[...].reshape(128, DL), jnp.concatenate([hot_more, jnp.zeros_like(hot_more)], axis=1))
    attend(1)
    attend(2)
    prepare(3)
    add(*landed(3, 0))
    add(*landed(3, 1, (0,)))
    last = landed(3, 1, (1,))
    for half in (0, 1):
        part = pl.ds(256 * half, 256)
        add(*last, part)
        lat_out[part] = (acc[part] * (1.0 / total[part])).astype(jnp.bfloat16)
        for p in range(max(1, 16 * half), 16 * half + 16):
            pltpu.make_async_remote_copy(
                src_ref=lat_out.at[pl.ds(16 * p, 16)],
                dst_ref=lat_in.at[pl.ds(pl.multiple_of(me * 16, 16), 16)],
                send_sem=o_ss, recv_sem=o_rs, **to(behind(me, OFFSETS[p]))
            ).start()
    lat_in[own, :] = lat_out[pl.ds(0, 16), :]
    settled(lat_in.at[pl.ds(0, 496)], o_ss, o_rs).wait_recv()
    loads[3].wait()
    got = lat_in[...]
    result = jnp.zeros((512, 128), jnp.float32)
    for h in range(4):
        result = jnp.where(row % 4 == h, jnp.dot(got, absorb_v[h], preferred_element_type=jnp.float32), result)
    out[...] = result.astype(jnp.bfloat16)

    settled(ids_in.at[pl.ds(1, 7)], ids_ss, ids_rs).wait_send()
    settled(q_out.at[pl.ds(0, 496)], q_ss, q_rs).wait_send()
    for copy in own_up[0] + own_up[1] + own_down[0] + own_down[1] + on_up + on_down:
        copy.wait_send()
    for w in range(4):
        settled(stage_turn.at[w, pl.ds(1, 7)], t_ss.at[w], t_rs.at[w]).wait_send()
        for i in (0, 1):
            settled(stage.at[w, i, pl.ds(1, 7)], k_ss.at[w, i], k_rs.at[w, i]).wait_send()
    settled(lat_out.at[pl.ds(0, 496)], o_ss, o_rs).wait_send()

    @pl.when(me == N - 1)
    def _():
        for copy in across:
            copy.wait_send()

    @pl.when((y == 3) & (c == 1))
    def _():
        for copy in down:
            copy.wait_send()

    @pl.when(c == 1)
    def _():
        for copy in over:
            copy.wait_send()


def body(query, absorb_k, absorb_v, latent_cache, cold_blocks):
    vmem = pl.BlockSpec(memory_space=pltpu.VMEM)
    bf16, f32, i32 = jnp.bfloat16, jnp.float32, jnp.int32
    dma = pltpu.SemaphoreType.DMA
    out = pl.pallas_call(
        kernel,
        out_shape=jax.ShapeDtypeStruct((512, 128), bf16),
        in_specs=[pl.BlockSpec(memory_space=pltpu.HBM)] * 4 + [vmem],
        out_specs=vmem,
        scratch_shapes=[
            pltpu.VMEM((4, 192, 128), bf16),
            pltpu.VMEM((512, DL), bf16),
            pltpu.VMEM((4, DL, 128), bf16),
            pltpu.VMEM((576, 1024), bf16),
            pltpu.VMEM((16, BLK, DL), bf16),
            pltpu.VMEM((16, BLK, DL), bf16),
            pltpu.VMEM((16, BLK, DL), bf16),
            pltpu.VMEM((16, BLK, DL), bf16),
            pltpu.VMEM((4, 16, BLK, 128), bf16),
            pltpu.VMEM((4, 8, BLK, 128), bf16),
            pltpu.VMEM((N, 1, 128), i32),
            pltpu.VMEM((8, 4, 1, 128), i32),
            pltpu.SMEM((8, 4, 1, 128), i32),
            pltpu.VMEM((2, N, 128), f32),
            pltpu.VMEM((512, 640), bf16),
            pltpu.VMEM((512, 768), bf16),
            pltpu.VMEM((4, 2, 8, BLK, DL), bf16),
            pltpu.VMEM((4, 8, 16, DL), bf16),
            pltpu.VMEM((4, 2, 8, BLK, DL), bf16),
            pltpu.VMEM((4, 8, 16, DL), bf16),
            pltpu.VMEM((2, BLK, DL), bf16),
            pltpu.VMEM((16, DL), bf16),
            pltpu.VMEM((4, 2, 8, BLK, 256), bf16),
            pltpu.VMEM((512, 1), f32),
            pltpu.VMEM((512, 1), f32),
            pltpu.VMEM((512, DL), f32),
            pltpu.VMEM((512, DL), bf16),
            pltpu.VMEM((512, DL), bf16),
        ]
        + [dma, dma, dma((2, 2, 2)), dma((2, 2, 2)), dma((2, 2)), dma((2, 2)), dma, dma]
        + [dma((4, 2)), dma((4, 3)), dma((4,)), dma((4,)), dma, dma]
        + [dma((2, 7)), dma((2,)), dma, dma((4,)), pltpu.SemaphoreType.REGULAR],
        compiler_params=pltpu.CompilerParams(collective_id=0, has_side_effects=True, vmem_limit_bytes=64 * 2**20 - 160 * 2**10),
    )(
        query.transpose(1, 2, 0),
        absorb_k.reshape(512, DL),
        absorb_v,
        latent_cache.T,
        cold_blocks,
    )
    return out.reshape(128, 4, 128)


def solution(mesh):
    placed = (
        P("grp", "ctx", None),
        P("ctx", None, None),
        P("ctx", None, None),
        P("ctx", None),
        P(("grp", "ctx"), None),
    )
    return jax.shard_map(
        body, mesh=mesh, in_specs=placed, out_specs=P("grp", "ctx", None), check_vma=False
    )
```

```python
import functools
import math

import jax
import jax.numpy as jnp
from jax import lax
from jax.experimental import pallas as pl
from jax.experimental.pallas import tpu as pltpu
from jax.sharding import PartitionSpec as P

MESH = pl.DeviceIdType.MESH
DL = 512
DN = 128
BLK = 64
N = 32
NEG = -1e30

AXIS = (0, 3, 1, 2)
SERVED = ((0, 2), (0, 1), (0, 3), (1, 2), (1, 1), (1, 3), (1, 0))

RINGS = (
    ((2, 2),),
    ((2, 1), (1, 2), (2, 3), (3, 2)),
    ((1, 1), (3, 3), (1, 3), (3, 1)),
    ((2, 0), (0, 2)),
    ((1, 0), (0, 1), (3, 0), (0, 3)),
)
OFFSETS = [(0, 0, 0)]
for ring in RINGS:
    for core in (0, 1):
        OFFSETS += [(dx, dy, core) for dx, dy in ring]
OFFSETS.append((0, 0, 1))


def ahead(me, offset):
    dx, dy, dc = offset
    x, y, c = me // 8, (me // 2) % 4, me % 2
    return (((x + dx) % 4) * 4 + (y + dy) % 4) * 2 + (c + dc) % 2


def behind(me, offset):
    dx, dy, dc = offset
    return ahead(me, ((4 - dx) % 4, (4 - dy) % 4, dc))


def to(device):
    return dict(device_id={"ctx": device}, device_id_type=MESH)


def pack(rows, rope, id0, id1, first, second, turns):
    first[...] = rows[id0]
    second[...] = rows[id1]
    lane = lax.broadcasted_iota(jnp.int32, (BLK, 128), 1)
    both = jnp.where(lane < 64, rope[id0], rope[id1])
    for b in range(4):
        turns[:, pl.ds(128 * b, 128)] = both[16 * b : 16 * b + 16]


def kernel(
    query_at, absorb_k_at, absorb_v_at, stored_at, cold_at, out,
    query, absorb_k, absorb_v, stored, cold,
    rows0, rows1, rows2, rows3, rope, pairs, ids_out, ids_in, ids, bias, q_out, q_all, stage, stage_turn, keys, keys_turn, hot, hot_turn, extra,
    top, total, acc, lat_out, lat_in, values,
    ids_ss, ids_rs, own_ss, own_rs, fwd_ss, fwd_rs, q_ss, q_rs, k_ss, k_rs, t_ss, t_rs, o_ss, o_rs, hot_ss, hot_rs, id_sem, in_sem, all_in,
):
    me = lax.axis_index("ctx")
    x, y, c = me // 8, (me // 2) % 4, me % 2

    def place(core):
        return jnp.where(core == 0, y, x), jnp.where(core == 0, x, y)

    def device(core, u, v):
        return (jnp.where(core == 0, v, u) * 4 + jnp.where(core == 0, u, v)) * 2 + core

    u, v = place(c)
    rows = (rows0, rows1, rows2, rows3)
    plus, minus = device(c, u, (v + 1) % 4), device(c, u, (v + 3) % 4)

    def served(flip, e):
        return device(c, (u + e) % 4, v) - c + (c + flip) % 2

    def server(flip, e):
        core = (c + flip) % 2
        cu, cv = place(core)
        return device(core, (cu + 4 - e) % 4, cv), core * 16 + (cu + 4 - e) % 4 * 4, cv

    barrier = pltpu.get_barrier_semaphore()
    crossing = [offset for offset in OFFSETS[1:] if 0 in offset[:2]]
    for offset in crossing:
        pl.semaphore_signal(barrier, inc=1, **to(ahead(me, offset)))

    loads = [
        pltpu.make_async_copy(src, dst, in_sem.at[k])
        for k, (src, dst) in enumerate(
            (
                (stored_at, stored), (query_at, query), (absorb_k_at, absorb_k), (absorb_v_at, absorb_v),
                (cold_at, cold),
            )
        )
    ]
    for load in loads:
        load.start()

    loads[4].wait()
    line = lax.broadcasted_iota(jnp.int32, (N, 1), 0)
    core, cu, cv = line // 16, (line // 4) % 4, line % 4
    base = jnp.where(core == 0, cv * 8 + cu * 2, cu * 8 + cv * 2 + 1) * 16
    local = [cold[r : r + 1, :] - base for r in range(4)]
    low, high = None, None
    for r in range(4):
        inside = (local[r] >= 0) & (local[r] < 16)
        a = jnp.min(jnp.where(inside, local[r], 99), axis=1, keepdims=True)
        b = jnp.max(jnp.where(inside, local[r], -1), axis=1, keepdims=True)
        low = a if r == 0 else jnp.minimum(low, a)
        high = b if r == 0 else jnp.maximum(high, b)
    id0 = jnp.where(high < 0, 0, low)
    id1 = jnp.where(high < 0, 0, high)
    lane = lax.broadcasted_iota(jnp.int32, (N, 128), 1)
    ids_out[...] = jnp.where(lane == 0, id0, id1).reshape(N, 1, 128)
    for s, wanted in ((0, id0), (1, id1)):
        mark = jnp.zeros((N, 128), jnp.float32)
        for r in range(4):
            found = jnp.max(jnp.where(local[r] == wanted, 1, 0), axis=1, keepdims=True)
            if s == 1:
                found = jnp.where(id1 == id0, 0, found)
            mark = jnp.where((lane == r) & (found == 0), NEG, mark)
        bias[s] = mark

    lanes = (((1,), (1,)), ((), ()))
    unit = jnp.where(
        lax.broadcasted_iota(jnp.int32, (256, 256), 0) == lax.broadcasted_iota(jnp.int32, (256, 256), 1), 1.0, 0.0
    ).astype(jnp.bfloat16)
    loads[0].wait()
    for k in range(4):
        part = pl.ds(256 * k, 256)
        turned = lax.dot_general(unit, stored[:DL, part], lanes, preferred_element_type=jnp.float32)
        rows[0][pl.ds(4 * k, 4)] = turned.astype(jnp.bfloat16).reshape(4, BLK, DL)
        tail = stored[DL:, part]
        turned = lax.dot_general(
            unit, jnp.concatenate([tail, tail], axis=0), lanes, preferred_element_type=jnp.float32
        )
        rope[0, pl.ds(4 * k, 4)] = turned.astype(jnp.bfloat16).reshape(4, BLK, 128)
    low_lanes = lax.broadcasted_iota(jnp.int32, (8, BLK, 128), 2) < 64
    pairs[0] = jnp.where(low_lanes, rope[0, pl.ds(0, 8)], rope[0, pl.ds(8, 8)])

    pl.semaphore_wait(barrier, len(crossing))
    for offset in crossing:
        pl.semaphore_signal(all_in, inc=1, **to(ahead(me, offset)))
    for flip, e in SERVED:
        there, first_row, _ = server(flip, e)
        pltpu.make_async_remote_copy(
            src_ref=ids_out.at[pl.ds(first_row, 4)], dst_ref=ids_in.at[4 * flip + e],
            send_sem=ids_ss, recv_sem=ids_rs, **to(there)
        ).start()
    ids_in[0] = ids_out[pl.ds(c * 16 + u * 4, 4)]

    def settled(ref, sends, lands):
        return pltpu.make_async_remote_copy(src_ref=ref, dst_ref=ref, send_sem=sends, recv_sem=lands, **to(ahead(me, OFFSETS[1])))

    def hot_copies(k, offset):
        device = to(ahead(me, offset))
        return [
            pltpu.make_async_remote_copy(
                src_ref=ref, dst_ref=ref, send_sem=hot_ss.at[i, k], recv_sem=hot_rs.at[i], **device
            )
            for i, ref in enumerate((hot, hot_turn))
        ]

    across = hot_copies(0, (1, 0, 0)) + hot_copies(1, (2, 0, 0)) + hot_copies(2, (3, 0, 0))
    down = hot_copies(3, (0, 1, 0)) + hot_copies(4, (0, 2, 0)) + hot_copies(5, (0, 3, 0))
    over = hot_copies(6, (0, 0, 1))

    @pl.when(me == N - 1)
    def _():
        pack(rows[0], rope.at[0], 14, 15, hot.at[0], hot.at[1], hot_turn)
        for copy in across + down:
            copy.start()

    def hop(src, dst, half, there, sends, lands):
        span, turns = pl.ds(8 * half, 8), pl.ds(4 * half, 4)
        return [
            pltpu.make_async_remote_copy(
                src_ref=a, dst_ref=b, send_sem=sends.at[i], recv_sem=lands.at[i], **to(there)
            )
            for i, (a, b) in enumerate(
                ((rows[src].at[span], rows[dst].at[span]), (pairs.at[src, turns], pairs.at[dst, turns]))
            )
        ]

    own_up = [hop(0, 1, h, plus, own_ss.at[0, h], own_rs.at[0, h]) for h in (0, 1)]
    own_down = [hop(0, 2, h, minus, own_ss.at[1, h], own_rs.at[1, h]) for h in (0, 1)]
    on_up = hop(1, 3, 0, plus, fwd_ss.at[0], fwd_rs.at[0])
    on_down = hop(2, 3, 1, minus, fwd_ss.at[1], fwd_rs.at[1])

    def start(*groups):
        for copies in groups:
            for copy in copies:
                copy.start()

    def arrive(*groups):
        for copies in groups:
            for copy in copies:
                copy.wait_recv()

    start(own_up[0], own_down[1])

    row = lax.broadcasted_iota(jnp.int32, (512, 128), 0)
    column = lax.broadcasted_iota(jnp.int32, (512, 128), 1)
    plain, turn = [], None
    loads[1].wait()
    loads[2].wait()
    for h in range(4):
        pick = jnp.where(row == 4 * column + h, 1.0, 0.0).astype(jnp.bfloat16)
        spread = lax.dot_general(pick, query[h], lanes, preferred_element_type=jnp.float32)
        plain.append(spread[:, :DN].astype(jnp.bfloat16))
        turn = spread[:, DN:] if h == 0 else turn + spread[:, DN:]
    q_out[:, :DL] = jnp.dot(
        jnp.concatenate(plain, axis=1), absorb_k[...], preferred_element_type=jnp.float32
    ).astype(jnp.bfloat16)
    turn = turn.astype(jnp.bfloat16)
    q_out[:, DL:] = jnp.concatenate([turn, turn], axis=1)
    pl.semaphore_wait(all_in, len(crossing))
    for p in range(1, N):
        dst = ahead(me, OFFSETS[p])
        pltpu.make_async_remote_copy(
            src_ref=q_out.at[pl.ds(pl.multiple_of(dst * 16, 16), 16)],
            dst_ref=q_all.at[pl.ds(16 * p, 16), pl.ds(0, 640)],
            send_sem=q_ss, recv_sem=q_rs, **to(dst)
        ).start()

    @pl.when((y == 3) & (c == 1) & (x != 3))
    def _():
        arrive(across[:2])
        start(down)

    start(own_up[1], own_down[0])

    settled(ids_in.at[pl.ds(1, 7)], ids_ss, ids_rs).wait_recv()
    fetch = pltpu.make_async_copy(ids_in, ids, id_sem)
    fetch.start()
    fetch.wait()

    def serve(w):
        at = (v + AXIS[w]) % 4
        for flip, e in SERVED:
            j = 4 * flip + e
            pack(
                rows[w], rope.at[w], ids[j, at, 0, 0], ids[j, at, 0, 1],
                stage.at[w, 0, j], stage.at[w, 1, j], stage_turn.at[w, j]
            )
            there = to(served(flip, e))
            pltpu.make_async_remote_copy(
                src_ref=stage_turn.at[w, j], dst_ref=keys_turn.at[w, j],
                send_sem=t_ss.at[w], recv_sem=t_rs.at[w], **there
            ).start()
            pltpu.make_async_remote_copy(
                src_ref=stage.at[w, 0, j], dst_ref=keys.at[w, 0, j],
                send_sem=k_ss.at[w, 0], recv_sem=k_rs.at[w, 0], **there
            ).start()
        for flip, e in SERVED:
            j = 4 * flip + e
            pltpu.make_async_remote_copy(
                src_ref=stage.at[w, 1, j], dst_ref=keys.at[w, 1, j],
                send_sem=k_ss.at[w, 1], recv_sem=k_rs.at[w, 1 + flip], **to(served(flip, e))
            ).start()
        pack(
            rows[w], rope.at[w], ids[0, at, 0, 0], ids[0, at, 0, 1],
            keys.at[w, 0, 0], keys.at[w, 1, 0], keys_turn.at[w, 0]
        )

    def widen(w):
        both = pairs[w]
        for half in (0, 1):
            one = both[:, :, 64 * half : 64 * half + 64]
            rope[w, pl.ds(8 * half, 8)] = jnp.concatenate([one, one], axis=2)

    serve(0)
    arrive(own_up[0], own_down[1])
    start(on_up, on_down)

    own = pl.ds(pl.multiple_of(me * 16, 16), 16)
    q_all[pl.ds(0, 16), pl.ds(0, 640)] = q_out[own, :]
    marks = (lax.broadcasted_iota(jnp.int32, (512, 128), 0) // 4) % 4 == lax.broadcasted_iota(
        jnp.int32, (512, 128), 1
    )
    q_all[:, 640:] = jnp.where(marks, 1.0, 0.0).astype(jnp.bfloat16)
    for flip in (0, 1):
        for e in range(4):
            _, first_row, at = server(flip, e)
            for w in range(4):
                for i in (0, 1):
                    mark = bias[i, pl.ds(first_row + (at + AXIS[w]) % 4, 1), :]
                    extra[w, i, 4 * flip + e, :, pl.ds(128, 128)] = jnp.broadcast_to(mark, (BLK, 128)).astype(
                        jnp.bfloat16
                    )
    arrive(own_up[1])
    widen(1)

    @pl.when((c == 1) & (y != 3))
    def _():
        arrive(down[:2])

    @pl.when(c == 1)
    def _():
        start(over)

    serve(1)
    arrive(own_down[0])
    widen(2)
    serve(2)

    scale = math.log2(math.e) / math.sqrt(192)
    first = lax.broadcasted_iota(jnp.int32, (BLK, 128), 1) < 64
    none = jnp.zeros((BLK, 128), jnp.bfloat16)

    def unpack(turns):
        both = jnp.concatenate([turns[:, 128 * b : 128 * b + 128] for b in range(4)], axis=0)
        return jnp.where(first, both, none), jnp.where(first, none, both)

    def add(latent, more, part=slice(None)):
        s = lax.dot_general(q_all[part, :DL], latent, lanes, preferred_element_type=jnp.float32)
        s += lax.dot_general(q_all[part, DL:], more, lanes, preferred_element_type=jnp.float32)
        s *= scale
        old = top[part]
        new = jnp.maximum(old, jnp.max(s, axis=1, keepdims=True))
        fade = jnp.exp2(old - new)
        w = jnp.exp2(s - new)
        total[part] = total[part] * fade + jnp.sum(w, axis=1, keepdims=True)
        top[part] = new
        acc[part] = acc[part] * fade + jnp.dot(
            w.astype(jnp.bfloat16), latent, preferred_element_type=jnp.float32
        )

    top[...] = jnp.full((512, 1), NEG, jnp.float32)
    total[...] = jnp.zeros((512, 1), jnp.float32)
    acc[...] = jnp.zeros((512, DL), jnp.float32)

    def prepare(w):
        settled(keys_turn.at[w, pl.ds(1, 7)], t_ss.at[w], t_rs.at[w]).wait_recv()
        for j in range(8):
            for i, turned in enumerate(unpack(keys_turn[w, j])):
                extra[w, i, j, :, pl.ds(0, 128)] = turned

    def landed(w, i, flips=(0, 1)):
        for flip in flips if i else (0,):
            span = pl.ds(4 * flip + 1 - flip, 3 + flip) if i else pl.ds(1, 7)
            settled(keys.at[w, i, span], k_ss.at[w, i], k_rs.at[w, i + flip]).wait_recv()
        run = pl.ds(4 * flips[0], 4 * len(flips))
        tokens = 256 * len(flips)
        return keys[w, i, run].reshape(tokens, DL), extra[w, i, run].reshape(tokens, 256)

    def attend(w):
        prepare(w)
        for i in (0, 1):
            add(*landed(w, i))

    settled(q_all.at[pl.ds(16, 496), pl.ds(0, 640)], q_ss, q_rs).wait_recv()
    attend(0)
    arrive(on_up, on_down)
    widen(3)
    serve(3)

    @pl.when(c == 0)
    def _():
        arrive(over)

    hot_more = jnp.concatenate(unpack(hot_turn[...]), axis=0)
    add(hot[...].reshape(128, DL), jnp.concatenate([hot_more, jnp.zeros_like(hot_more)], axis=1))
    loads[3].wait()
    for h in range(4):
        values[:, pl.ds(128 * h, 128)] = absorb_v[h]
    attend(1)
    attend(2)
    prepare(3)
    add(*landed(3, 0))
    add(*landed(3, 1, (0,)))
    last = landed(3, 1, (1,))
    for half in (0, 1):
        part = pl.ds(256 * half, 256)
        add(*last, part)
        lat_out[part] = (acc[part] * (1.0 / total[part])).astype(jnp.bfloat16)
        for p in range(max(1, 16 * half), 16 * half + 16):
            pltpu.make_async_remote_copy(
                src_ref=lat_out.at[pl.ds(16 * p, 16)],
                dst_ref=lat_in.at[pl.ds(pl.multiple_of(me * 16, 16), 16)],
                send_sem=o_ss, recv_sem=o_rs, **to(behind(me, OFFSETS[p]))
            ).start()
    lat_in[own, :] = lat_out[pl.ds(0, 16), :]
    settled(lat_in.at[pl.ds(0, 496)], o_ss, o_rs).wait_recv()
    got = lat_in[...]
    wide = jnp.dot(got, values[...], preferred_element_type=jnp.float32)
    result = wide[:, :128]
    for h in range(1, 4):
        result = jnp.where(row % 4 == h, wide[:, 128 * h : 128 * h + 128], result)
    out[...] = result.astype(jnp.bfloat16)

    settled(ids_in.at[pl.ds(1, 7)], ids_ss, ids_rs).wait_send()
    settled(q_out.at[pl.ds(0, 496)], q_ss, q_rs).wait_send()
    for copy in own_up[0] + own_up[1] + own_down[0] + own_down[1] + on_up + on_down:
        copy.wait_send()
    for w in range(4):
        settled(stage_turn.at[w, pl.ds(1, 7)], t_ss.at[w], t_rs.at[w]).wait_send()
        for i in (0, 1):
            settled(stage.at[w, i, pl.ds(1, 7)], k_ss.at[w, i], k_rs.at[w, i]).wait_send()
    settled(lat_out.at[pl.ds(0, 496)], o_ss, o_rs).wait_send()

    @pl.when(me == N - 1)
    def _():
        for copy in across:
            copy.wait_send()

    @pl.when((y == 3) & (c == 1))
    def _():
        for copy in down:
            copy.wait_send()

    @pl.when(c == 1)
    def _():
        for copy in over:
            copy.wait_send()


def body(query, absorb_k, absorb_v, latent_cache, cold_blocks):
    vmem = pl.BlockSpec(memory_space=pltpu.VMEM)
    bf16, f32, i32 = jnp.bfloat16, jnp.float32, jnp.int32
    dma = pltpu.SemaphoreType.DMA
    out = pl.pallas_call(
        kernel,
        out_shape=jax.ShapeDtypeStruct((512, 128), bf16),
        in_specs=[pl.BlockSpec(memory_space=pltpu.HBM)] * 5,
        out_specs=vmem,
        scratch_shapes=[
            pltpu.VMEM((4, 192, 128), bf16),
            pltpu.VMEM((512, DL), bf16),
            pltpu.VMEM((4, DL, 128), bf16),
            pltpu.VMEM((576, 1024), bf16),
            pltpu.VMEM((4, 30), i32),
            pltpu.VMEM((16, BLK, DL), bf16),
            pltpu.VMEM((16, BLK, DL), bf16),
            pltpu.VMEM((16, BLK, DL), bf16),
            pltpu.VMEM((16, BLK, DL), bf16),
            pltpu.VMEM((4, 16, BLK, 128), bf16),
            pltpu.VMEM((4, 8, BLK, 128), bf16),
            pltpu.VMEM((N, 1, 128), i32),
            pltpu.VMEM((8, 4, 1, 128), i32),
            pltpu.SMEM((8, 4, 1, 128), i32),
            pltpu.VMEM((2, N, 128), f32),
            pltpu.VMEM((512, 640), bf16),
            pltpu.VMEM((512, 768), bf16),
            pltpu.VMEM((4, 2, 8, BLK, DL), bf16),
            pltpu.VMEM((4, 8, 16, DL), bf16),
            pltpu.VMEM((4, 2, 8, BLK, DL), bf16),
            pltpu.VMEM((4, 8, 16, DL), bf16),
            pltpu.VMEM((2, BLK, DL), bf16),
            pltpu.VMEM((16, DL), bf16),
            pltpu.VMEM((4, 2, 8, BLK, 256), bf16),
            pltpu.VMEM((512, 1), f32),
            pltpu.VMEM((512, 1), f32),
            pltpu.VMEM((512, DL), f32),
            pltpu.VMEM((512, DL), bf16),
            pltpu.VMEM((512, DL), bf16),
            pltpu.VMEM((DL, 512), bf16),
        ]
        + [dma, dma, dma((2, 2, 2)), dma((2, 2, 2)), dma((2, 2)), dma((2, 2)), dma, dma]
        + [dma((4, 2)), dma((4, 3)), dma((4,)), dma((4,)), dma, dma]
        + [dma((2, 7)), dma((2,)), dma, dma((5,)), pltpu.SemaphoreType.REGULAR],
        compiler_params=pltpu.CompilerParams(collective_id=0, has_side_effects=True, vmem_limit_bytes=64 * 2**20 - 160 * 2**10),
    )(
        query.transpose(1, 2, 0),
        absorb_k.reshape(512, DL),
        absorb_v,
        latent_cache.T,
        cold_blocks,
    )
    return out.reshape(128, 4, 128)


def solution(mesh):
    placed = (
        P("grp", "ctx", None),
        P("ctx", None, None),
        P("ctx", None, None),
        P("ctx", None),
        P(("grp", "ctx"), None),
    )
    return jax.shard_map(
        body, mesh=mesh, in_specs=placed, out_specs=P("grp", "ctx", None), check_vma=False
    )
```

```python
import functools
import math

import jax
import jax.numpy as jnp
from jax import lax
from jax.experimental import pallas as pl
from jax.experimental.pallas import tpu as pltpu
from jax.sharding import PartitionSpec as P

MESH = pl.DeviceIdType.MESH
DL = 512
DN = 128
BLK = 64
N = 32
NEG = -1e30

AXIS = (0, 3, 1, 2)
SERVED = ((0, 2), (0, 1), (0, 3), (1, 2), (1, 1), (1, 3), (1, 0))

RINGS = (
    ((2, 2),),
    ((2, 1), (1, 2), (2, 3), (3, 2)),
    ((1, 1), (3, 3), (1, 3), (3, 1)),
    ((2, 0), (0, 2)),
    ((1, 0), (0, 1), (3, 0), (0, 3)),
)
OFFSETS = [(0, 0, 0)]
for ring in RINGS:
    for core in (0, 1):
        OFFSETS += [(dx, dy, core) for dx, dy in ring]
OFFSETS.append((0, 0, 1))


def ahead(me, offset):
    dx, dy, dc = offset
    x, y, c = me // 8, (me // 2) % 4, me % 2
    return (((x + dx) % 4) * 4 + (y + dy) % 4) * 2 + (c + dc) % 2


def behind(me, offset):
    dx, dy, dc = offset
    return ahead(me, ((4 - dx) % 4, (4 - dy) % 4, dc))


def to(device):
    return dict(device_id={"ctx": device}, device_id_type=MESH)


def pack(rows, rope, id0, id1, first, second, turns):
    first[...] = rows[id0]
    second[...] = rows[id1]
    lane = lax.broadcasted_iota(jnp.int32, (BLK, 128), 1)
    both = jnp.where(lane < 64, rope[id0], rope[id1])
    for b in range(4):
        turns[:, pl.ds(128 * b, 128)] = both[16 * b : 16 * b + 16]


def kernel(
    query_at, absorb_k_at, absorb_v_at, stored_at, cold_at, out,
    query, absorb_k, absorb_v, stored, cold,
    rows0, rows1, rows2, rows3, rope, pairs, ids_out, ids_in, ids, bias, q_out, q_all, stage, stage_turn, keys, keys_turn, hot, hot_turn, extra,
    top, total, acc, lat_out, lat_in, values,
    ids_ss, ids_rs, own_ss, own_rs, fwd_ss, fwd_rs, q_ss, q_rs, k_ss, k_rs, t_ss, t_rs, o_ss, o_rs, hot_ss, hot_rs, id_sem, in_sem, all_in,
):
    me = lax.axis_index("ctx")
    x, y, c = me // 8, (me // 2) % 4, me % 2

    def place(core):
        return jnp.where(core == 0, y, x), jnp.where(core == 0, x, y)

    def device(core, u, v):
        return (jnp.where(core == 0, v, u) * 4 + jnp.where(core == 0, u, v)) * 2 + core

    u, v = place(c)
    rows = (rows0, rows1, rows2, rows3)
    plus, minus = device(c, u, (v + 1) % 4), device(c, u, (v + 3) % 4)

    def served(flip, e):
        return device(c, (u + e) % 4, v) - c + (c + flip) % 2

    def server(flip, e):
        core = (c + flip) % 2
        cu, cv = place(core)
        return device(core, (cu + 4 - e) % 4, cv), core * 16 + (cu + 4 - e) % 4 * 4, cv

    barrier = pltpu.get_barrier_semaphore()
    crossing = [offset for offset in OFFSETS[1:] if 0 in offset[:2]]
    for offset in crossing:
        pl.semaphore_signal(barrier, inc=1, **to(ahead(me, offset)))

    loads = [
        pltpu.make_async_copy(src, dst, in_sem.at[k])
        for k, (src, dst) in enumerate(
            [(stored_at.at[:, pl.ds(256 * n, 256)], stored.at[:, pl.ds(256 * n, 256)]) for n in range(4)]
            + [(query_at, query), (absorb_k_at, absorb_k), (absorb_v_at, absorb_v), (cold_at, cold)]
        )
    ]
    for load in loads[7:] + loads[:7]:
        load.start()

    loads[7].wait()
    line = lax.broadcasted_iota(jnp.int32, (N, 1), 0)
    core, cu, cv = line // 16, (line // 4) % 4, line % 4
    base = jnp.where(core == 0, cv * 8 + cu * 2, cu * 8 + cv * 2 + 1) * 16
    local = [cold[r : r + 1, :] - base for r in range(4)]
    low, high = None, None
    for r in range(4):
        inside = (local[r] >= 0) & (local[r] < 16)
        a = jnp.min(jnp.where(inside, local[r], 99), axis=1, keepdims=True)
        b = jnp.max(jnp.where(inside, local[r], -1), axis=1, keepdims=True)
        low = a if r == 0 else jnp.minimum(low, a)
        high = b if r == 0 else jnp.maximum(high, b)
    id0 = jnp.where(high < 0, 0, low)
    id1 = jnp.where(high < 0, 0, high)
    lane = lax.broadcasted_iota(jnp.int32, (N, 128), 1)
    ids_out[...] = jnp.where(lane == 0, id0, id1).reshape(N, 1, 128)
    for s, wanted in ((0, id0), (1, id1)):
        mark = jnp.zeros((N, 128), jnp.float32)
        for r in range(4):
            found = jnp.max(jnp.where(local[r] == wanted, 1, 0), axis=1, keepdims=True)
            if s == 1:
                found = jnp.where(id1 == id0, 0, found)
            mark = jnp.where((lane == r) & (found == 0), NEG, mark)
        bias[s] = mark

    lanes = (((1,), (1,)), ((), ()))
    unit = jnp.where(
        lax.broadcasted_iota(jnp.int32, (256, 256), 0) == lax.broadcasted_iota(jnp.int32, (256, 256), 1), 1.0, 0.0
    ).astype(jnp.bfloat16)
    for k in range(4):
        loads[k].wait()
        part = pl.ds(256 * k, 256)
        turned = lax.dot_general(unit, stored[:DL, part], lanes, preferred_element_type=jnp.float32)
        rows[0][pl.ds(4 * k, 4)] = turned.astype(jnp.bfloat16).reshape(4, BLK, DL)
        tail = stored[DL:, part]
        turned = lax.dot_general(
            unit, jnp.concatenate([tail, tail], axis=0), lanes, preferred_element_type=jnp.float32
        )
        rope[0, pl.ds(4 * k, 4)] = turned.astype(jnp.bfloat16).reshape(4, BLK, 128)
    low_lanes = lax.broadcasted_iota(jnp.int32, (8, BLK, 128), 2) < 64
    pairs[0] = jnp.where(low_lanes, rope[0, pl.ds(0, 8)], rope[0, pl.ds(8, 8)])

    pl.semaphore_wait(barrier, len(crossing))
    for offset in crossing:
        pl.semaphore_signal(all_in, inc=1, **to(ahead(me, offset)))
    for flip, e in SERVED:
        there, first_row, _ = server(flip, e)
        pltpu.make_async_remote_copy(
            src_ref=ids_out.at[pl.ds(first_row, 4)], dst_ref=ids_in.at[4 * flip + e],
            send_sem=ids_ss, recv_sem=ids_rs, **to(there)
        ).start()
    ids_in[0] = ids_out[pl.ds(c * 16 + u * 4, 4)]

    def settled(ref, sends, lands):
        return pltpu.make_async_remote_copy(src_ref=ref, dst_ref=ref, send_sem=sends, recv_sem=lands, **to(ahead(me, OFFSETS[1])))

    def hot_copies(k, offset):
        device = to(ahead(me, offset))
        return [
            pltpu.make_async_remote_copy(
                src_ref=ref, dst_ref=ref, send_sem=hot_ss.at[i, k], recv_sem=hot_rs.at[i], **device
            )
            for i, ref in enumerate((hot, hot_turn))
        ]

    across = hot_copies(0, (1, 0, 0)) + hot_copies(1, (2, 0, 0)) + hot_copies(2, (3, 0, 0))
    down = hot_copies(3, (0, 1, 0)) + hot_copies(4, (0, 2, 0)) + hot_copies(5, (0, 3, 0))
    over = hot_copies(6, (0, 0, 1))

    @pl.when(me == N - 1)
    def _():
        pack(rows[0], rope.at[0], 14, 15, hot.at[0], hot.at[1], hot_turn)
        for copy in across + down:
            copy.start()

    def hop(src, dst, half, there, sends, lands):
        span, turns = pl.ds(8 * half, 8), pl.ds(4 * half, 4)
        return [
            pltpu.make_async_remote_copy(
                src_ref=a, dst_ref=b, send_sem=sends.at[i], recv_sem=lands.at[i], **to(there)
            )
            for i, (a, b) in enumerate(
                ((rows[src].at[span], rows[dst].at[span]), (pairs.at[src, turns], pairs.at[dst, turns]))
            )
        ]

    own_up = [hop(0, 1, h, plus, own_ss.at[0, h], own_rs.at[0, h]) for h in (0, 1)]
    own_down = [hop(0, 2, h, minus, own_ss.at[1, h], own_rs.at[1, h]) for h in (0, 1)]
    on_up = hop(1, 3, 0, plus, fwd_ss.at[0], fwd_rs.at[0])
    on_down = hop(2, 3, 1, minus, fwd_ss.at[1], fwd_rs.at[1])

    def start(*groups):
        for copies in groups:
            for copy in copies:
                copy.start()

    def arrive(*groups):
        for copies in groups:
            for copy in copies:
                copy.wait_recv()

    start(own_up[0], own_down[1])

    row = lax.broadcasted_iota(jnp.int32, (512, 128), 0)
    column = lax.broadcasted_iota(jnp.int32, (512, 128), 1)
    plain, turn = [], None
    loads[4].wait()
    loads[5].wait()
    for h in range(4):
        pick = jnp.where(row == 4 * column + h, 1.0, 0.0).astype(jnp.bfloat16)
        spread = lax.dot_general(pick, query[h], lanes, preferred_element_type=jnp.float32)
        plain.append(spread[:, :DN].astype(jnp.bfloat16))
        turn = spread[:, DN:] if h == 0 else turn + spread[:, DN:]
    q_out[:, :DL] = jnp.dot(
        jnp.concatenate(plain, axis=1), absorb_k[...], preferred_element_type=jnp.float32
    ).astype(jnp.bfloat16)
    turn = turn.astype(jnp.bfloat16)
    q_out[:, DL:] = jnp.concatenate([turn, turn], axis=1)
    pl.semaphore_wait(all_in, len(crossing))
    for p in range(1, N):
        dst = ahead(me, OFFSETS[p])
        pltpu.make_async_remote_copy(
            src_ref=q_out.at[pl.ds(pl.multiple_of(dst * 16, 16), 16)],
            dst_ref=q_all.at[pl.ds(16 * p, 16), pl.ds(0, 640)],
            send_sem=q_ss, recv_sem=q_rs, **to(dst)
        ).start()

    @pl.when((y == 3) & (c == 1) & (x != 3))
    def _():
        arrive(across[:2])
        start(down)

    start(own_up[1], own_down[0])

    settled(ids_in.at[pl.ds(1, 7)], ids_ss, ids_rs).wait_recv()
    fetch = pltpu.make_async_copy(ids_in, ids, id_sem)
    fetch.start()
    fetch.wait()

    def serve(w):
        at = (v + AXIS[w]) % 4
        for flip, e in SERVED:
            j = 4 * flip + e
            pack(
                rows[w], rope.at[w], ids[j, at, 0, 0], ids[j, at, 0, 1],
                stage.at[w, 0, j], stage.at[w, 1, j], stage_turn.at[w, j]
            )
            there = to(served(flip, e))
            pltpu.make_async_remote_copy(
                src_ref=stage_turn.at[w, j], dst_ref=keys_turn.at[w, j],
                send_sem=t_ss.at[w], recv_sem=t_rs.at[w], **there
            ).start()
            pltpu.make_async_remote_copy(
                src_ref=stage.at[w, 0, j], dst_ref=keys.at[w, 0, j],
                send_sem=k_ss.at[w, 0], recv_sem=k_rs.at[w, 0], **there
            ).start()
        for flip, e in SERVED:
            j = 4 * flip + e
            pltpu.make_async_remote_copy(
                src_ref=stage.at[w, 1, j], dst_ref=keys.at[w, 1, j],
                send_sem=k_ss.at[w, 1], recv_sem=k_rs.at[w, 1 + flip], **to(served(flip, e))
            ).start()
        pack(
            rows[w], rope.at[w], ids[0, at, 0, 0], ids[0, at, 0, 1],
            keys.at[w, 0, 0], keys.at[w, 1, 0], keys_turn.at[w, 0]
        )

    def widen(w):
        both = pairs[w]
        for half in (0, 1):
            one = both[:, :, 64 * half : 64 * half + 64]
            rope[w, pl.ds(8 * half, 8)] = jnp.concatenate([one, one], axis=2)

    serve(0)
    arrive(own_up[0], own_down[1])
    start(on_up, on_down)

    own = pl.ds(pl.multiple_of(me * 16, 16), 16)
    q_all[pl.ds(0, 16), pl.ds(0, 640)] = q_out[own, :]
    marks = (lax.broadcasted_iota(jnp.int32, (512, 128), 0) // 4) % 4 == lax.broadcasted_iota(
        jnp.int32, (512, 128), 1
    )
    q_all[:, 640:] = jnp.where(marks, 1.0, 0.0).astype(jnp.bfloat16)
    for flip in (0, 1):
        for e in range(4):
            _, first_row, at = server(flip, e)
            for w in range(4):
                for i in (0, 1):
                    mark = bias[i, pl.ds(first_row + (at + AXIS[w]) % 4, 1), :]
                    extra[w, i, 4 * flip + e, :, pl.ds(128, 128)] = jnp.broadcast_to(mark, (BLK, 128)).astype(
                        jnp.bfloat16
                    )
    arrive(own_up[1])
    widen(1)

    @pl.when((c == 1) & (y != 3))
    def _():
        arrive(down[:2])

    @pl.when(c == 1)
    def _():
        start(over)

    serve(1)
    arrive(own_down[0])
    widen(2)
    serve(2)

    scale = math.log2(math.e) / math.sqrt(192)
    first = lax.broadcasted_iota(jnp.int32, (BLK, 128), 1) < 64
    none = jnp.zeros((BLK, 128), jnp.bfloat16)

    def unpack(turns):
        both = jnp.concatenate([turns[:, 128 * b : 128 * b + 128] for b in range(4)], axis=0)
        return jnp.where(first, both, none), jnp.where(first, none, both)

    def add(latent, more, part=slice(None)):
        s = lax.dot_general(q_all[part, :DL], latent, lanes, preferred_element_type=jnp.float32)
        s += lax.dot_general(q_all[part, DL:], more, lanes, preferred_element_type=jnp.float32)
        s *= scale
        old = top[part]
        new = jnp.maximum(old, jnp.max(s, axis=1, keepdims=True))
        fade = jnp.exp2(old - new)
        w = jnp.exp2(s - new)
        total[part] = total[part] * fade + jnp.sum(w, axis=1, keepdims=True)
        top[part] = new
        acc[part] = acc[part] * fade + jnp.dot(
            w.astype(jnp.bfloat16), latent, preferred_element_type=jnp.float32
        )

    top[...] = jnp.full((512, 1), NEG, jnp.float32)
    total[...] = jnp.zeros((512, 1), jnp.float32)
    acc[...] = jnp.zeros((512, DL), jnp.float32)

    def prepare(w):
        settled(keys_turn.at[w, pl.ds(1, 7)], t_ss.at[w], t_rs.at[w]).wait_recv()
        for j in range(8):
            for i, turned in enumerate(unpack(keys_turn[w, j])):
                extra[w, i, j, :, pl.ds(0, 128)] = turned

    def landed(w, i, flips=(0, 1)):
        for flip in flips if i else (0,):
            span = pl.ds(4 * flip + 1 - flip, 3 + flip) if i else pl.ds(1, 7)
            settled(keys.at[w, i, span], k_ss.at[w, i], k_rs.at[w, i + flip]).wait_recv()
        run = pl.ds(4 * flips[0], 4 * len(flips))
        tokens = 256 * len(flips)
        return keys[w, i, run].reshape(tokens, DL), extra[w, i, run].reshape(tokens, 256)

    def attend(w):
        prepare(w)
        for i in (0, 1):
            add(*landed(w, i))

    settled(q_all.at[pl.ds(16, 496), pl.ds(0, 640)], q_ss, q_rs).wait_recv()
    attend(0)
    arrive(on_up, on_down)
    widen(3)
    serve(3)

    @pl.when(c == 0)
    def _():
        arrive(over)

    hot_more = jnp.concatenate(unpack(hot_turn[...]), axis=0)
    add(hot[...].reshape(128, DL), jnp.concatenate([hot_more, jnp.zeros_like(hot_more)], axis=1))
    loads[6].wait()
    for h in range(4):
        values[:, pl.ds(128 * h, 128)] = absorb_v[h]
    attend(1)
    attend(2)
    prepare(3)
    add(*landed(3, 0))
    add(*landed(3, 1, (0,)))
    last = landed(3, 1, (1,))
    for half in (0, 1):
        part = pl.ds(256 * half, 256)
        add(*last, part)
        lat_out[part] = (acc[part] * (1.0 / total[part])).astype(jnp.bfloat16)
        for p in range(max(1, 16 * half), 16 * half + 16):
            pltpu.make_async_remote_copy(
                src_ref=lat_out.at[pl.ds(16 * p, 16)],
                dst_ref=lat_in.at[pl.ds(pl.multiple_of(me * 16, 16), 16)],
                send_sem=o_ss, recv_sem=o_rs, **to(behind(me, OFFSETS[p]))
            ).start()
    lat_in[own, :] = lat_out[pl.ds(0, 16), :]
    settled(lat_in.at[pl.ds(0, 496)], o_ss, o_rs).wait_recv()
    got = lat_in[...]
    wide = jnp.dot(got, values[...], preferred_element_type=jnp.float32)
    result = wide[:, :128]
    for h in range(1, 4):
        result = jnp.where(row % 4 == h, wide[:, 128 * h : 128 * h + 128], result)
    out[...] = result.astype(jnp.bfloat16)

    settled(ids_in.at[pl.ds(1, 7)], ids_ss, ids_rs).wait_send()
    settled(q_out.at[pl.ds(0, 496)], q_ss, q_rs).wait_send()
    for copy in own_up[0] + own_up[1] + own_down[0] + own_down[1] + on_up + on_down:
        copy.wait_send()
    for w in range(4):
        settled(stage_turn.at[w, pl.ds(1, 7)], t_ss.at[w], t_rs.at[w]).wait_send()
        for i in (0, 1):
            settled(stage.at[w, i, pl.ds(1, 7)], k_ss.at[w, i], k_rs.at[w, i]).wait_send()
    settled(lat_out.at[pl.ds(0, 496)], o_ss, o_rs).wait_send()

    @pl.when(me == N - 1)
    def _():
        for copy in across:
            copy.wait_send()

    @pl.when((y == 3) & (c == 1))
    def _():
        for copy in down:
            copy.wait_send()

    @pl.when(c == 1)
    def _():
        for copy in over:
            copy.wait_send()


def body(query, absorb_k, absorb_v, latent_cache, cold_blocks):
    vmem = pl.BlockSpec(memory_space=pltpu.VMEM)
    bf16, f32, i32 = jnp.bfloat16, jnp.float32, jnp.int32
    dma = pltpu.SemaphoreType.DMA
    out = pl.pallas_call(
        kernel,
        out_shape=jax.ShapeDtypeStruct((512, 128), bf16),
        in_specs=[pl.BlockSpec(memory_space=pltpu.HBM)] * 5,
        out_specs=vmem,
        scratch_shapes=[
            pltpu.VMEM((4, 192, 128), bf16),
            pltpu.VMEM((512, DL), bf16),
            pltpu.VMEM((4, DL, 128), bf16),
            pltpu.VMEM((576, 1024), bf16),
            pltpu.VMEM((4, 30), i32),
            pltpu.VMEM((16, BLK, DL), bf16),
            pltpu.VMEM((16, BLK, DL), bf16),
            pltpu.VMEM((16, BLK, DL), bf16),
            pltpu.VMEM((16, BLK, DL), bf16),
            pltpu.VMEM((4, 16, BLK, 128), bf16),
            pltpu.VMEM((4, 8, BLK, 128), bf16),
            pltpu.VMEM((N, 1, 128), i32),
            pltpu.VMEM((8, 4, 1, 128), i32),
            pltpu.SMEM((8, 4, 1, 128), i32),
            pltpu.VMEM((2, N, 128), f32),
            pltpu.VMEM((512, 640), bf16),
            pltpu.VMEM((512, 768), bf16),
            pltpu.VMEM((4, 2, 8, BLK, DL), bf16),
            pltpu.VMEM((4, 8, 16, DL), bf16),
            pltpu.VMEM((4, 2, 8, BLK, DL), bf16),
            pltpu.VMEM((4, 8, 16, DL), bf16),
            pltpu.VMEM((2, BLK, DL), bf16),
            pltpu.VMEM((16, DL), bf16),
            pltpu.VMEM((4, 2, 8, BLK, 256), bf16),
            pltpu.VMEM((512, 1), f32),
            pltpu.VMEM((512, 1), f32),
            pltpu.VMEM((512, DL), f32),
            pltpu.VMEM((512, DL), bf16),
            pltpu.VMEM((512, DL), bf16),
            pltpu.VMEM((DL, 512), bf16),
        ]
        + [dma, dma, dma((2, 2, 2)), dma((2, 2, 2)), dma((2, 2)), dma((2, 2)), dma, dma]
        + [dma((4, 2)), dma((4, 3)), dma((4,)), dma((4,)), dma, dma]
        + [dma((2, 7)), dma((2,)), dma, dma((8,)), pltpu.SemaphoreType.REGULAR],
        compiler_params=pltpu.CompilerParams(collective_id=0, has_side_effects=True, vmem_limit_bytes=64 * 2**20 - 160 * 2**10),
    )(
        query.transpose(1, 2, 0),
        absorb_k.reshape(512, DL),
        absorb_v,
        latent_cache.T,
        cold_blocks,
    )
    return out.reshape(128, 4, 128)


def solution(mesh):
    placed = (
        P("grp", "ctx", None),
        P("ctx", None, None),
        P("ctx", None, None),
        P("ctx", None),
        P(("grp", "ctx"), None),
    )
    return jax.shard_map(
        body, mesh=mesh, in_specs=placed, out_specs=P("grp", "ctx", None), check_vma=False
    )
```
